512 devices in a mesh: seq: 128 (over z, y, core), mp: 4 (over x).
Axes of the slice: x: 4, y: 4, z: 16, core: 2. Of those that a mesh axis runs over, the one named last changes fastest.
Arguments:
- queries: bfloat16 [8, 16384], P(None, ('mp', 'seq')), may hold values from -200 to 200
- new_keys: bfloat16 [8, 1024], P(None, 'mp'), may hold values from -4 to 4
- new_values: bfloat16 [8, 1024], P(None, 'mp'), may hold values from -6 to 6
- keys: bfloat16 [512, 512, 1024], P('seq', None, 'mp'), may hold values from -5 to 5
- values: bfloat16 [512, 512, 1024], P('seq', None, 'mp'), may hold values from -6 to 6
- page_table: int32 [8, 64], replicated, may hold values from 0 to 511, as said below
- lengths: int32 [8], replicated, may hold values from 7682 to 32768, as said below
- out_weight: bfloat16 [16384, 16384], P('mp', 'seq'), may hold values from -0.046875 to 0.046875
Outputs:
- mixed: bfloat16 [8, 16384], P(None, 'seq')
The draws below stay inside these ranges and needn't reach their ends.
Inputs may be any that keep to these rules, and one draw needn't show every extreme that they name: `page_table`: each of the 512 slot numbers appears exactly once in the table. Slot n is local slot n % 4 of the device with index n // 4 along seq. Row r keeps its tokens in the slots of its first ceil(lengths[r] / 512) entries, in order; the slots of its other entries hold no live token. `lengths`: some row has exactly 32768 cached tokens.
All inputs are finite; a program needn't handle non-finite values.
Results may differ from the reference program's by a relative error of at most 0.0051.
Values may be sent and summed in bfloat16 or wider, within the bound.
A program may use at most 64 MiB of HBM per device.

```python
import math
import jax
import jax.numpy as jnp
from jax import lax

D = 16384
QH = 128
KVH = 8
HD = 128
GROUP = 16
PAGE = 512
ROWS = 8
SLOTS_ALL = 512
PAGES_ROW = 64


def table_draw(key):
    folded = jax.random.fold_in(key, 101)
    order_key, count_key, pick_key, tail_key = jax.random.split(folded, 4)
    slot_order = jax.random.permutation(order_key, SLOTS_ALL).astype(jnp.int32).reshape(ROWS, PAGES_ROW)
    lowest = max(1, PAGES_ROW // 4)
    counts = jax.random.randint(count_key, (ROWS,), lowest, PAGES_ROW + 1, dtype=jnp.int32)
    chosen_row = jax.random.randint(pick_key, (), 0, ROWS, dtype=jnp.int32)
    marker = jnp.arange(ROWS, dtype=jnp.int32) == chosen_row
    counts = jnp.where(marker, PAGES_ROW, counts)
    tail_lengths = jax.random.randint(tail_key, (ROWS,), 2, PAGE + 1, dtype=jnp.int32)
    tail_lengths = jnp.where(marker, PAGE, tail_lengths)
    return (slot_order, ((counts - 1) * PAGE + tail_lengths).astype(jnp.int32))


def fresh_keys(key):
    folded = jax.random.fold_in(key, 202)
    return jnp.clip(jax.random.normal(folded, (ROWS, KVH * HD), jnp.float32), -4.0, 4.0)


def new_key_factor(key):
    folded = jax.random.fold_in(key, 303)
    offset = jax.random.randint(folded, (), 0, 2, dtype=jnp.int32)
    pattern = (jnp.arange(ROWS, dtype=jnp.int32)[:, None] + jnp.arange(KVH, dtype=jnp.int32)[None, :] + offset) % 2
    factor = jnp.where(pattern == 1, -0.5, 1.0).astype(jnp.float32)
    return jnp.repeat(factor, HD, axis=1)


def draw_page_table(key, part):
    slot_order, spans = table_draw(key)
    return slot_order


def draw_lengths(key, part):
    slot_order, spans = table_draw(key)
    return spans


def draw_new_keys(key, part):
    shared = fresh_keys(key)
    factor = new_key_factor(key)
    return (shared * factor).astype(jnp.bfloat16)


def draw_queries(key, part):
    shared = fresh_keys(key).reshape(ROWS, KVH, 1, HD)
    key = jax.random.fold_in(key, 5)
    spread_key, pull_key = jax.random.split(key)
    pull_strength = jax.random.uniform(pull_key, (ROWS, KVH, GROUP, 1), jnp.float32, 9.0, 12.0)
    ladder = jnp.arange(ROWS, dtype=jnp.float32) / max(ROWS - 1, 1)
    leading = (jnp.arange(GROUP) == 0).reshape(1, 1, GROUP, 1)
    spread_part = jnp.clip(jax.random.normal(spread_key, (ROWS, KVH, GROUP, HD), jnp.float32), -6.0, 6.0) * 2.5
    strong = (120.0 + 100.0 * ladder).reshape(ROWS, 1, 1, 1)
    pull_strength = jnp.where(leading, strong, pull_strength)
    return (spread_part + pull_strength * shared / HD ** 0.5).reshape(ROWS, QH * HD).astype(jnp.bfloat16)


def draw_keys(key, part):
    slot_order, spans = table_draw(key)
    shared = fresh_keys(key)
    key = jax.random.fold_in(key, 7)
    value_key = jax.random.fold_in(key, 0)
    cache_shape = (SLOTS_ALL, PAGE, KVH * HD)
    cache_values = jnp.clip(jax.random.normal(value_key, cache_shape, jnp.float32), -5.0, 5.0)
    first_pages = slot_order[:, 0]
    owner_hits = (jnp.arange(SLOTS_ALL, dtype=jnp.int32)[:, None] == first_pages[None, :]).astype(jnp.float32)
    planted = jnp.sum(owner_hits[:, :, None] * shared[None, :, :], axis=1)
    holder = jnp.sum(owner_hits, axis=1)[:, None] > 0.5
    cache_values = cache_values.at[:, 0, :].set(jnp.where(holder, planted, cache_values[:, 0, :]))
    cache_values = cache_values.at[:, 1, :].set(jnp.where(holder, planted * 1.01, cache_values[:, 1, :]))
    return cache_values.astype(jnp.bfloat16)


def levels(key, extent, cuts, low, largest):
    def one(axis_at, blocks):
        steps = jax.random.uniform(jax.random.fold_in(jax.random.fold_in(key, 6), axis_at), (blocks,), jnp.float32, low / len(cuts), largest / len(cuts))
        return jnp.repeat(jnp.exp(steps), extent[axis_at] // blocks).reshape((-1,) + (1,) * (len(extent) - axis_at - 1))

    level = one(*cuts[0])
    for cut in cuts[1:]:
        level = level * one(*cut)
    return level


def gaussian(stream_key, extent, width, most, shards=(), kind=jnp.bfloat16):
    values = width * jax.random.normal(stream_key, extent, jnp.float32)
    if shards:
        values = values * levels(stream_key, extent, shards, -0.22, 0.18)
    return jnp.clip(values, -most, most).astype(kind)


def setup_inputs(seed: int = 0) -> dict:
    seeds = jax.random.split(jax.random.key(seed), 9)
    queries = draw_queries(jax.random.fold_in(seeds[8], 71), 0)
    new_keys = draw_new_keys(jax.random.fold_in(seeds[8], 71), 0)
    new_values = gaussian(seeds[2], (ROWS, KVH * HD), 1.0, 6.0, ((1, 4),))
    keys = draw_keys(jax.random.fold_in(seeds[8], 71), 0)
    values = gaussian(seeds[4], (SLOTS_ALL, PAGE, KVH * HD), 1.0, 6.0, ((0, 128), (2, 4)))
    page_table = draw_page_table(jax.random.fold_in(seeds[8], 71), 0)
    lengths = draw_lengths(jax.random.fold_in(seeds[8], 71), 0)
    out_weight = gaussian(seeds[7], (QH * HD, D), (QH * HD) ** -0.5, 0.046875, ((0, 4), (1, 128)))
    return dict(queries=queries, new_keys=new_keys, new_values=new_values, keys=keys, values=values, page_table=page_table, lengths=lengths, out_weight=out_weight)


NEG = -1e+30

def merge_states(earlier, later):
    highest = jnp.maximum(earlier[0], later[0])
    early_scale = jnp.exp(earlier[0] - highest)
    late_scale = jnp.exp(later[0] - highest)
    return (highest, earlier[1] * early_scale + later[1] * late_scale, earlier[2] * early_scale[..., None] + later[2] * late_scale[..., None])

def page_state(query_heads, key_page, value_page, live_mask):
    scores = jnp.einsum('kgd,tkd->kgt', query_heads.astype(jnp.float32), key_page.astype(jnp.float32)) / math.sqrt(HD)
    masked = jnp.where(live_mask[None, None, :], scores, NEG)
    highest = lax.optimization_barrier(jnp.max(masked, axis=2))
    weights = jnp.where(live_mask[None, None, :], jnp.exp(masked - highest[..., None]), 0.0)
    page_total = lax.optimization_barrier(jnp.sum(weights, axis=2))
    rounded = weights.astype(jnp.bfloat16)
    output = jnp.einsum('kgt,tkd->kgd', rounded.astype(jnp.float32), value_page.astype(jnp.float32))
    return (highest, page_total, output)

def reference(queries, new_keys, new_values, keys, values, page_table, lengths, out_weight):
    offsets = jnp.arange(PAGE, dtype=jnp.int32)

    def one_row(row_index):
        query_heads = queries[row_index].reshape(KVH, GROUP, HD)
        row_length = lengths[row_index]
        slot_list = page_table[row_index]
        start_state = (jnp.full((KVH, GROUP), NEG, jnp.float32), jnp.zeros((KVH, GROUP), jnp.float32), jnp.zeros((KVH, GROUP, HD), jnp.float32))

        def add_page(carried, page_index):
            slot_index = slot_list[page_index].astype(jnp.int32)
            key_page = lax.dynamic_index_in_dim(keys, slot_index, 0, keepdims=False).reshape(PAGE, KVH, HD)
            value_page = lax.dynamic_index_in_dim(values, slot_index, 0, keepdims=False).reshape(PAGE, KVH, HD)
            live_mask = page_index * PAGE + offsets < row_length
            return (merge_states(carried, page_state(query_heads, key_page, value_page, live_mask)), None)
        carried, unused = lax.scan(add_page, start_state, jnp.arange(PAGES_ROW, dtype=jnp.int32))
        new_key = new_keys[row_index].reshape(KVH, HD)
        new_scores = jnp.einsum('kgd,kd->kg', query_heads.astype(jnp.float32), new_key.astype(jnp.float32)) / math.sqrt(HD)
        fresh = (new_scores, jnp.ones((KVH, GROUP), jnp.float32), jnp.broadcast_to(new_values[row_index].reshape(KVH, 1, HD).astype(jnp.float32), (KVH, GROUP, HD)))
        highest, row_total, row_out = merge_states(carried, fresh)
        return (row_out / row_total[..., None]).reshape(QH * HD).astype(jnp.bfloat16)
    attended = lax.map(one_row, jnp.arange(ROWS, dtype=jnp.int32))
    return jnp.dot(attended, out_weight, preferred_element_type=jnp.float32).astype(jnp.bfloat16)
```

```python
import math

import jax
import jax.numpy as jnp
from jax import lax
from jax.experimental import pallas as pl
from jax.experimental.pallas import tpu as pltpu
from jax.sharding import PartitionSpec as P

MESH = pl.DeviceIdType.MESH
NEG = -1e30
HD = 128
ROWS = 8
PLANES = 16
LOCAL = 8
XS = 4
SLOTS = 4
PAGE = 512
F32 = jnp.float32
BF16 = jnp.bfloat16


def iota(shape, axis):
    return lax.broadcasted_iota(jnp.int32, shape, axis)


def kernel(
    q_ref, nk_ref, nv_ref, pt_ref, len_ref, k_hbm, v_hbm, w_hbm, out_ref,
    k_buf, v_buf, w_buf, zq, qbuf, sbuf, rbuf, zo, zs, abuf, xbuf,
    load_sem, send_sem, recv_sem,
):
    i = lax.axis_index("seq")
    x = lax.axis_index("mp")
    z = i // LOCAL
    p = lax.rem(i, LOCAL)

    z_steps = sorted(range(1, PLANES), key=lambda k: -min(k, PLANES - k))
    p_steps = (4, 5, 2, 3, 6, 7, 1)
    x_steps = (2, 1, 3)

    def z_peer(k):
        return {"seq": lax.rem(z + k, PLANES) * LOCAL + p}

    def p_index(k):
        return lax.rem(p + k, LOCAL)

    def p_peer(k):
        return {"seq": z * LOCAL + p_index(k)}

    def x_peer(k):
        return {"mp": lax.rem(x + k, XS)}

    peers = [z_peer(k) for k in z_steps]
    peers += [p_peer(k) for k in p_steps]
    peers += [x_peer(k) for k in x_steps]
    barrier = pltpu.get_barrier_semaphore()
    for peer in peers:
        pl.semaphore_signal(barrier, inc=1, device_id=peer, device_id_type=MESH)

    loads = [
        pltpu.make_async_copy(src, dst, load_sem.at[n])
        for n, (src, dst) in enumerate(((k_hbm, k_buf), (v_hbm, v_buf), (w_hbm, w_buf)))
    ]
    for load in loads:
        load.start()

    def send(src, dst, n, peer):
        pltpu.make_async_remote_copy(
            src_ref=src, dst_ref=dst, send_sem=send_sem.at[n], recv_sem=recv_sem.at[n],
            device_id=peer, device_id_type=MESH,
        ).start()

    def wait(ref, sems, n):
        pltpu.make_async_copy(ref, ref, sems.at[n]).wait()

    spread = (iota((32, 128), 0) == (iota((32, 128), 1) & 31)).astype(BF16)
    wide = jnp.dot(q_ref[...], spread, preferred_element_type=F32)
    row8 = iota((8, 128), 0)
    mine = jnp.where((iota((8, 128), 1) >> 5) == (row8 & 3), wide, 0.0)
    low = jnp.sum(jnp.where(row8 < 4, mine, 0.0), axis=0, keepdims=True)
    high = jnp.sum(jnp.where(row8 < 4, 0.0, mine), axis=0, keepdims=True)
    zq[z] = jnp.where(row8 == 0, low, jnp.where(row8 == 1, high, 0.0))

    pl.semaphore_wait(barrier, len(peers))
    for k in z_steps:
        send(zq.at[z], zq.at[z], 0, z_peer(k))

    lane64 = iota((128, 64), 1)
    rho = iota((128, 64), 0)
    my_slot = i * SLOTS + ((rho >> 2) & 3)
    plane_slot = z * (LOCAL * SLOTS) + (rho >> 2)
    row_acc = jnp.zeros((128, 64), F32)
    live_acc = jnp.zeros((128, 64), F32)
    plane_acc = jnp.zeros((128, 64), F32)
    for r in range(ROWS):
        entry = pt_ref[r : r + 1, :]
        hit = entry == my_slot
        row_acc += jnp.where(hit, float(r), 0.0)
        live_acc += jnp.where(hit, (len_ref[r] - lane64 * PAGE).astype(F32), 0.0)
        plane_acc += jnp.where(entry == plane_slot, float(r), 0.0)
    row_of = jnp.sum(row_acc, axis=1, keepdims=True).astype(jnp.int32)
    live_of = jnp.sum(live_acc, axis=1, keepdims=True).astype(jnp.int32)
    plane_row = jnp.sum(plane_acc, axis=1, keepdims=True).astype(jnp.int32)

    rho1 = iota((128, 1), 0)
    tau1 = iota((32, 1), 0)
    head = jnp.concatenate([4 * (rho1 >> 4) + (rho1 & 3), 4 * p + (tau1 >> 3)], axis=0)
    row = jnp.concatenate([row_of, tau1 & 7], axis=0)
    start = (head & 1) * 128 + (row >> 2) * 16 + (head >> 1)
    column = iota((160, 256), 1)
    select = jnp.concatenate(
        [(column == start + quarter * 32).astype(F32) for quarter in range(4)], axis=0
    ).astype(BF16)
    lane160 = iota((160, 128), 1)
    in_row = (lane160 >> 5) == (row & 3)
    l0, l1 = iota((128, 128), 0), iota((128, 128), 1)
    same = (l0 & 31) == (l1 & 31)
    fold = [(same & ((l1 >> 5) == quarter)).astype(F32).astype(BF16) for quarter in range(4)]
    slot_of = (rho1 >> 2) & 3
    match = ((l0 & 3) == ((l1 >> 3) & 3)) & (plane_row == (l1 & 7))
    first_kv = p < 4
    nk = jnp.where(first_kv, nk_ref[:, :HD].astype(F32), nk_ref[:, HD:].astype(F32))
    nv = jnp.where(first_kv, nv_ref[:, :HD].astype(F32), nv_ref[:, HD:].astype(F32))
    nk = jnp.concatenate([nk] * 4, axis=0)
    nv = jnp.concatenate([nv] * 4, axis=0)

    wait(zq.at[pl.ds(0, PLANES - 1)], recv_sem, 0)
    qbuf[p] = jnp.concatenate([zq[:, 0, :], zq[:, 1, :]], axis=0)
    for k in p_steps:
        send(qbuf.at[p], qbuf.at[p], 1, p_peer(k))
    wait(qbuf.at[pl.ds(0, LOCAL - 1)], recv_sem, 1)

    gathered = qbuf[...].reshape(256, 128).astype(BF16)
    picked = jnp.dot(select, gathered, preferred_element_type=F32)
    queries = jnp.zeros((160, 128), F32)
    for quarter in range(4):
        part = jnp.where(in_row, picked[quarter * 160 : (quarter + 1) * 160], 0.0).astype(BF16)
        queries += jnp.dot(part, fold[quarter], preferred_element_type=F32)
    fresh_queries = queries[128:]
    queries = queries[:128]

    loads[0].wait()
    scores = jnp.zeros((128, PAGE), F32)
    first_half = rho1 < 64
    for s in range(SLOTS):
        here = slot_of == s
        block = jnp.concatenate(
            [
                jnp.where(here & first_half, queries, 0.0),
                jnp.where(here & jnp.logical_not(first_half), queries, 0.0),
            ],
            axis=1,
        ).astype(BF16)
        scores += lax.dot_general(
            block, k_buf[s], (((1,), (1,)), ((), ())), preferred_element_type=F32
        )
    scale = 1.0 / math.sqrt(HD)
    live = iota((128, PAGE), 1) < live_of
    masked = jnp.where(live, scores * scale, NEG)
    page_max = jnp.max(masked, axis=1, keepdims=True)
    weights = jnp.where(live, jnp.exp(masked - page_max), 0.0)
    page_total = jnp.sum(weights, axis=1, keepdims=True)
    loads[1].wait()
    outs = jnp.zeros((128, 2 * HD), F32)
    for s in range(SLOTS):
        outs += jnp.dot(
            jnp.where(slot_of == s, weights, 0.0).astype(BF16), v_buf[s], preferred_element_type=F32
        )
    stats = jnp.where(l1 < 64, page_max, page_total)
    for n in range(LOCAL):
        half = n // 4
        sbuf[n, 0:16, :] = outs[n * 16 : (n + 1) * 16, half * HD : (half + 1) * HD]
        sbuf[n, 16:32, :] = stats[n * 16 : (n + 1) * 16]
    for k in p_steps:
        send(sbuf.at[p_index(k)], rbuf.at[p], 2, p_peer(k))
    rbuf[p] = sbuf[p]
    fresh_scores = jnp.sum(fresh_queries * nk, axis=1, keepdims=True) * scale
    wait(rbuf.at[pl.ds(0, LOCAL - 1)], recv_sem, 2)

    parts = rbuf[:, 0:16, :].reshape(128, 128)
    stats = rbuf[:, 16:32, :].reshape(128, 128)
    turned = pltpu.roll(stats, 64, 1)
    part_max = jnp.where(l1 < 64, stats, turned)
    part_total = jnp.where(l1 < 64, turned, stats)
    plane_max = jnp.max(jnp.where(match, part_max, NEG), axis=0, keepdims=True)
    factor = jnp.where(match, jnp.exp(part_max - plane_max), 0.0)
    plane_total = jnp.sum(factor * part_total, axis=0, keepdims=True)
    merged = jnp.dot(
        factor.T[:32], parts, preferred_element_type=F32, precision=lax.Precision.HIGHEST
    )
    zo[z] = merged.astype(BF16)
    lane1 = iota((1, 128), 1)
    zs[z] = jnp.where(lane1 < 32, plane_max, plane_total)
    for k in z_steps:
        send(zs.at[z], zs.at[z], 3, z_peer(k))
        send(zo.at[z], zo.at[z], 4, z_peer(k))
    wait(zs.at[pl.ds(0, PLANES - 1)], recv_sem, 3)
    wait(zo.at[pl.ds(0, PLANES - 1)], recv_sem, 4)

    table = jnp.full((128, 128), NEG, F32)
    for n in range(PLANES):
        table = jnp.where(l0 == n, zs[n], table)
    table = table.T
    lane32 = iota((32, 128), 1)
    maxima = jnp.where(lane32 < PLANES, table[:32], NEG)
    totals = jnp.where(lane32 < PLANES, table[32:64], 0.0)
    top = jnp.maximum(jnp.max(maxima, axis=1, keepdims=True), fresh_scores)
    factor = jnp.exp(maxima - top)
    fresh_factor = jnp.exp(fresh_scores - top)
    total = jnp.sum(factor * totals, axis=1, keepdims=True) + fresh_factor
    mixed = fresh_factor * nv
    for n in range(PLANES):
        mixed += factor[:, n : n + 1] * zo[n].astype(F32)
    abuf[p] = (mixed / total).astype(BF16)
    for k in p_steps:
        send(abuf.at[p], abuf.at[p], 5, p_peer(k))
    loads[2].wait()
    wait(abuf.at[pl.ds(0, LOCAL - 1)], recv_sem, 5)

    acc = jnp.zeros((ROWS, 128), F32)
    for n in range(LOCAL):
        block = abuf[n].astype(F32)
        flat = jnp.concatenate([block[8 * h : 8 * h + 8] for h in range(4)], axis=1).astype(BF16)
        acc += jnp.dot(flat, w_buf[n * 512 : (n + 1) * 512, :], preferred_element_type=F32)
    xbuf[x] = acc
    for k in x_steps:
        send(xbuf.at[x], xbuf.at[x], 6, x_peer(k))
    wait(xbuf.at[pl.ds(0, XS - 1)], recv_sem, 6)
    out_ref[...] = ((xbuf[0] + xbuf[1]) + (xbuf[2] + xbuf[3])).astype(out_ref.dtype)

    wait(zq.at[pl.ds(0, PLANES - 1)], send_sem, 0)
    wait(qbuf.at[pl.ds(0, LOCAL - 1)], send_sem, 1)
    wait(rbuf.at[pl.ds(0, LOCAL - 1)], send_sem, 2)
    wait(zs.at[pl.ds(0, PLANES - 1)], send_sem, 3)
    wait(zo.at[pl.ds(0, PLANES - 1)], send_sem, 4)
    wait(abuf.at[pl.ds(0, LOCAL - 1)], send_sem, 5)
    wait(xbuf.at[pl.ds(0, XS - 1)], send_sem, 6)


def shards(queries, new_keys, new_values, keys, values, page_table, lengths, out_weight):
    vmem = pl.BlockSpec(memory_space=pltpu.VMEM)
    smem = pl.BlockSpec(memory_space=pltpu.SMEM)
    hbm = pl.BlockSpec(memory_space=pl.ANY)
    return pl.pallas_call(
        kernel,
        out_shape=jax.ShapeDtypeStruct((ROWS, out_weight.shape[1]), BF16),
        in_specs=[vmem, vmem, vmem, vmem, smem, hbm, hbm, hbm],
        out_specs=vmem,
        scratch_shapes=[
            pltpu.VMEM(keys.shape, BF16),
            pltpu.VMEM(values.shape, BF16),
            pltpu.VMEM(out_weight.shape, BF16),
            pltpu.VMEM((PLANES, 8, 128), F32),
            pltpu.VMEM((LOCAL, 32, 128), F32),
            pltpu.VMEM((LOCAL, 32, 128), F32),
            pltpu.VMEM((LOCAL, 32, 128), F32),
            pltpu.VMEM((PLANES, 32, 128), BF16),
            pltpu.VMEM((PLANES, 1, 128), F32),
            pltpu.VMEM((LOCAL, 32, 128), BF16),
            pltpu.VMEM((XS, ROWS, 128), F32),
            pltpu.SemaphoreType.DMA((3,)),
            pltpu.SemaphoreType.DMA((7,)),
            pltpu.SemaphoreType.DMA((7,)),
        ],
        compiler_params=pltpu.CompilerParams(
            collective_id=0, has_side_effects=True, vmem_limit_bytes=48 * 1024 * 1024
        ),
    )(queries, new_keys, new_values, page_table, lengths, keys, values, out_weight)


def solution(mesh):
    placed = (
        P(None, ("mp", "seq")),
        P(None, "mp"),
        P(None, "mp"),
        P("seq", None, "mp"),
        P("seq", None, "mp"),
        P(),
        P(),
        P("mp", "seq"),
    )
    return jax.shard_map(
        shards, mesh=mesh, in_specs=placed, out_specs=P(None, "seq"), check_vma=False
    )
```

```python
import math

import jax
import jax.numpy as jnp
from jax import lax
from jax.experimental import pallas as pl
from jax.experimental.pallas import tpu as pltpu
from jax.sharding import PartitionSpec as P

MESH = pl.DeviceIdType.MESH
NEG = -1e30
HD = 128
ROWS = 8
PLANES = 16
LOCAL = 8
XS = 4
SLOTS = 4
PAGE = 512
F32 = jnp.float32
BF16 = jnp.bfloat16


def iota(shape, axis):
    return lax.broadcasted_iota(jnp.int32, shape, axis)


def kernel(
    q_hbm, nk_hbm, nv_hbm, pt_hbm, len_hbm, k_hbm, v_hbm, w_hbm, out_ref,
    q_ref, nk_ref, nv_ref, pt_ref, len_ref, k_buf, v_buf, w_buf, pbuf, zq, sbuf, rbuf, zo, zs, abuf, xbuf,
    load_sem, send_sem, recv_sem, ready_sem,
):
    i = lax.axis_index("seq")
    x = lax.axis_index("mp")
    z = i // LOCAL
    p = lax.rem(i, LOCAL)

    z_steps = sorted(range(1, PLANES), key=lambda k: -min(k, PLANES - k))
    p_steps = ((2, 0), (2, 1), (1, 0), (3, 0), (1, 1), (3, 1), (0, 1))
    x_steps = (2, 1, 3)

    def z_peer(k):
        return {"seq": lax.rem(z + k, PLANES) * LOCAL + p}

    def p_index(k):
        return lax.rem((p >> 1) + k[0], 4) * 2 + lax.rem((p & 1) + k[1], 2)

    def p_peer(k):
        return {"seq": z * LOCAL + p_index(k)}

    def x_peer(k):
        return {"mp": lax.rem(x + k, XS)}

    peers = [z_peer(k) for k in z_steps if min(k, PLANES - k) <= 4]
    peers += [p_peer(k) for k in p_steps]
    peers += [x_peer(k) for k in x_steps]
    barrier = pltpu.get_barrier_semaphore()
    for peer in peers:
        pl.semaphore_signal(barrier, inc=1, device_id=peer, device_id_type=MESH)

    loads = [
        pltpu.make_async_copy(src, dst, load_sem.at[n])
        for n, (src, dst) in enumerate(
            (
                (q_hbm, q_ref), (pt_hbm, pt_ref), (len_hbm, len_ref), (nk_hbm, nk_ref),
                (nv_hbm, nv_ref), (k_hbm, k_buf), (v_hbm, v_buf), (w_hbm, w_buf),
            )
        )
    ]
    for load in loads:
        load.start()

    def send(src, dst, n, peer, m=None):
        pltpu.make_async_remote_copy(
            src_ref=src, dst_ref=dst, send_sem=send_sem.at[n], recv_sem=recv_sem.at[n if m is None else m],
            device_id=peer, device_id_type=MESH,
        ).start()

    def wait(ref, sems, n):
        pltpu.make_async_copy(ref, ref, sems.at[n]).wait()

    loads[0].wait()
    lane8 = iota((8, 128), 1)
    spread = (iota((32, 128), 0) == (iota((32, 128), 1) & 31)).astype(BF16)
    wide = jnp.dot(q_ref[...], spread, preferred_element_type=F32)
    pbuf[p] = jnp.where((lane8 >> 5) == (p & 3), wide, 0.0)

    pl.semaphore_wait(barrier, len(peers))
    for k in (4, 12):
        pl.semaphore_signal(ready_sem, inc=1, device_id=z_peer(k), device_id_type=MESH)
    for k in p_steps:
        send(pbuf.at[p], pbuf.at[p], 0, p_peer(k))

    for load in loads[1:5]:
        load.wait()
    lane64 = iota((128, 64), 1)
    rho = iota((128, 64), 0)
    my_slot = i * SLOTS + ((rho >> 2) & 3)
    plane_slot = z * (LOCAL * SLOTS) + (rho >> 2)
    row_acc = jnp.zeros((128, 64), F32)
    live_acc = jnp.zeros((128, 64), F32)
    plane_acc = jnp.zeros((128, 64), F32)
    for r in range(ROWS):
        entry = pt_ref[r : r + 1, :]
        hit = entry == my_slot
        row_acc += jnp.where(hit, float(r), 0.0)
        live_acc += jnp.where(hit, (len_ref[r] - lane64 * PAGE).astype(F32), 0.0)
        plane_acc += jnp.where(entry == plane_slot, float(r), 0.0)
    row_of = jnp.sum(row_acc, axis=1, keepdims=True).astype(jnp.int32)
    live_of = jnp.sum(live_acc, axis=1, keepdims=True).astype(jnp.int32)
    plane_row = jnp.sum(plane_acc, axis=1, keepdims=True).astype(jnp.int32)

    rho1 = iota((128, 1), 0)
    tau1 = iota((32, 1), 0)
    head = jnp.concatenate([4 * (rho1 >> 4) + (rho1 & 3), 4 * p + (tau1 >> 3)], axis=0)
    row = jnp.concatenate([row_of, tau1 & 7], axis=0)
    start = (head >> 1) * 16 + (head & 1) * 8 + row
    select = (iota((160, 256), 1) == start).astype(F32).astype(BF16)
    l0, l1 = iota((128, 128), 0), iota((128, 128), 1)
    slot_of = (rho1 >> 2) & 3
    match = ((l0 & 3) == ((l1 >> 3) & 3)) & (plane_row == (l1 & 7))
    first_kv = p < 4
    nk = jnp.where(first_kv, nk_ref[:, :HD].astype(F32), nk_ref[:, HD:].astype(F32))
    nv = jnp.where(first_kv, nv_ref[:, :HD].astype(F32), nv_ref[:, HD:].astype(F32))
    nk = jnp.concatenate([nk] * 4, axis=0)
    nv = jnp.concatenate([nv] * 4, axis=0)

    wait(pbuf.at[pl.ds(0, LOCAL - 1)], recv_sem, 0)
    low = (pbuf[0] + pbuf[1]) + (pbuf[2] + pbuf[3])
    high = (pbuf[4] + pbuf[5]) + (pbuf[6] + pbuf[7])
    zq[z] = jnp.concatenate([low, high], axis=0).astype(BF16)
    pl.semaphore_wait(ready_sem, 2)
    for k in z_steps:
        send(zq.at[z], zq.at[z], 1, z_peer(k))
    wait(zq.at[pl.ds(0, PLANES - 1)], recv_sem, 1)

    queries = jnp.dot(select, zq[...].reshape(256, 128), preferred_element_type=F32)
    fresh_queries = queries[128:]
    queries = queries[:128]

    loads[5].wait()
    scores = jnp.zeros((128, PAGE), F32)
    first_half = rho1 < 64
    for s in range(SLOTS):
        here = slot_of == s
        block = jnp.concatenate(
            [
                jnp.where(here & first_half, queries, 0.0),
                jnp.where(here & jnp.logical_not(first_half), queries, 0.0),
            ],
            axis=1,
        ).astype(BF16)
        scores += lax.dot_general(
            block, k_buf[s], (((1,), (1,)), ((), ())), preferred_element_type=F32
        )
    scale = 1.0 / math.sqrt(HD)
    live = iota((128, PAGE), 1) < live_of
    masked = jnp.where(live, scores * scale, NEG)
    page_max = jnp.max(masked, axis=1, keepdims=True)
    weights = jnp.where(live, jnp.exp(masked - page_max), 0.0)
    page_total = jnp.sum(weights, axis=1, keepdims=True)
    loads[6].wait()
    outs = jnp.zeros((128, 2 * HD), F32)
    for s in range(SLOTS):
        outs += jnp.dot(
            jnp.where(slot_of == s, weights, 0.0).astype(BF16), v_buf[s], preferred_element_type=F32
        )
    stats = jnp.where(l1 < 64, page_max, page_total)
    for n in range(LOCAL):
        half = n // 4
        sbuf[n, 0:16, :] = outs[n * 16 : (n + 1) * 16, half * HD : (half + 1) * HD]
        sbuf[n, 16:32, :] = stats[n * 16 : (n + 1) * 16]
    for k in p_steps:
        send(sbuf.at[p_index(k)], rbuf.at[p], 2, p_peer(k))
    rbuf[p] = sbuf[p]
    fresh_scores = jnp.sum(fresh_queries * nk, axis=1, keepdims=True) * scale
    wait(rbuf.at[pl.ds(0, LOCAL - 1)], recv_sem, 2)

    parts = rbuf[:, 0:16, :].reshape(128, 128)
    stats = rbuf[:, 16:32, :].reshape(128, 128)
    turned = pltpu.roll(stats, 64, 1)
    part_max = jnp.where(l1 < 64, stats, turned)
    part_total = jnp.where(l1 < 64, turned, stats)
    plane_max = jnp.max(jnp.where(match, part_max, NEG), axis=0, keepdims=True)
    factor = jnp.where(match, jnp.exp(part_max - plane_max), 0.0)
    plane_total = jnp.sum(factor * part_total, axis=0, keepdims=True)
    merged = jnp.dot(
        factor.T[:32], parts, preferred_element_type=F32, precision=lax.Precision.HIGHEST
    )
    zo[z] = merged.astype(BF16)
    lane1 = iota((1, 128), 1)
    zs[z] = jnp.where(lane1 < 32, plane_max, plane_total)
    for k in z_steps:
        send(zs.at[z], zs.at[z], 3, z_peer(k))
        send(zo.at[z], zo.at[z], 4, z_peer(k))
    wait(zs.at[pl.ds(0, PLANES - 1)], recv_sem, 3)
    wait(zo.at[pl.ds(0, PLANES - 1)], recv_sem, 4)

    table = jnp.full((128, 128), NEG, F32)
    for n in range(PLANES):
        table = jnp.where(l0 == n, zs[n], table)
    table = table.T
    lane32 = iota((32, 128), 1)
    maxima = jnp.where(lane32 < PLANES, table[:32], NEG)
    totals = jnp.where(lane32 < PLANES, table[32:64], 0.0)
    top = jnp.maximum(jnp.max(maxima, axis=1, keepdims=True), fresh_scores)
    factor = jnp.exp(maxima - top)
    fresh_factor = jnp.exp(fresh_scores - top)
    total = jnp.sum(factor * totals, axis=1, keepdims=True) + fresh_factor
    mixed = fresh_factor * nv
    for n in range(PLANES):
        mixed += factor[:, n : n + 1] * zo[n].astype(F32)
    abuf[p] = (mixed / total).astype(BF16)
    for n, k in enumerate(p_steps):
        send(abuf.at[p], abuf.at[p], 5, p_peer(k), 7 + n)

    def project(n):
        block = abuf[n].astype(F32)
        flat = jnp.concatenate([block[8 * h : 8 * h + 8] for h in range(4)], axis=1).astype(BF16)
        rows = pl.ds(pl.multiple_of(n * 512, 512), 512)
        return jnp.dot(flat, w_buf[rows, :], preferred_element_type=F32)

    loads[7].wait()
    acc = project(p)
    for n, k in reversed(tuple(enumerate(p_steps))):
        source = p_index((4 - k[0], k[1]))
        wait(abuf.at[source], recv_sem, 7 + n)
        acc += project(source)
    xbuf[x] = acc
    for k in x_steps:
        send(xbuf.at[x], xbuf.at[x], 6, x_peer(k))
    wait(xbuf.at[pl.ds(0, XS - 1)], recv_sem, 6)
    out_ref[...] = ((xbuf[0] + xbuf[1]) + (xbuf[2] + xbuf[3])).astype(out_ref.dtype)

    wait(pbuf.at[pl.ds(0, LOCAL - 1)], send_sem, 0)
    wait(zq.at[pl.ds(0, PLANES - 1)], send_sem, 1)
    wait(rbuf.at[pl.ds(0, LOCAL - 1)], send_sem, 2)
    wait(zs.at[pl.ds(0, PLANES - 1)], send_sem, 3)
    wait(zo.at[pl.ds(0, PLANES - 1)], send_sem, 4)
    wait(abuf.at[pl.ds(0, LOCAL - 1)], send_sem, 5)
    wait(xbuf.at[pl.ds(0, XS - 1)], send_sem, 6)


def shards(queries, new_keys, new_values, keys, values, page_table, lengths, out_weight):
    vmem = pl.BlockSpec(memory_space=pltpu.VMEM)
    hbm = pl.BlockSpec(memory_space=pl.ANY)
    return pl.pallas_call(
        kernel,
        out_shape=jax.ShapeDtypeStruct((ROWS, out_weight.shape[1]), BF16),
        in_specs=[hbm] * 8,
        out_specs=vmem,
        scratch_shapes=[
            pltpu.VMEM(queries.shape, BF16),
            pltpu.VMEM(new_keys.shape, BF16),
            pltpu.VMEM(new_values.shape, BF16),
            pltpu.VMEM(page_table.shape, jnp.int32),
            pltpu.SMEM(lengths.shape, jnp.int32),
            pltpu.VMEM(keys.shape, BF16),
            pltpu.VMEM(values.shape, BF16),
            pltpu.VMEM(out_weight.shape, BF16),
            pltpu.VMEM((LOCAL, 8, 128), F32),
            pltpu.VMEM((PLANES, 16, 128), BF16),
            pltpu.VMEM((LOCAL, 32, 128), F32),
            pltpu.VMEM((LOCAL, 32, 128), F32),
            pltpu.VMEM((PLANES, 32, 128), BF16),
            pltpu.VMEM((PLANES, 1, 128), F32),
            pltpu.VMEM((LOCAL, 32, 128), BF16),
            pltpu.VMEM((XS, ROWS, 128), F32),
            pltpu.SemaphoreType.DMA((8,)),
            pltpu.SemaphoreType.DMA((7,)),
            pltpu.SemaphoreType.DMA((14,)),
            pltpu.SemaphoreType.REGULAR,
        ],
        compiler_params=pltpu.CompilerParams(
            collective_id=0, has_side_effects=True, vmem_limit_bytes=64 * 1024 * 1024
        ),
    )(queries, new_keys, new_values, page_table, lengths, keys, values, out_weight)


def solution(mesh):
    placed = (
        P(None, ("mp", "seq")),
        P(None, "mp"),
        P(None, "mp"),
        P("seq", None, "mp"),
        P("seq", None, "mp"),
        P(),
        P(),
        P("mp", "seq"),
    )
    return jax.shard_map(
        shards, mesh=mesh, in_specs=placed, out_specs=P(None, "seq"), check_vma=False
    )
```

```python
import math

import jax
import jax.numpy as jnp
from jax import lax
from jax.experimental import pallas as pl
from jax.experimental.pallas import tpu as pltpu
from jax.sharding import PartitionSpec as P

MESH = pl.DeviceIdType.MESH
NEG = -1e30
HD = 128
ROWS = 8
PLANES = 16
LOCAL = 8
XS = 4
SLOTS = 4
PAGE = 512
F32 = jnp.float32
BF16 = jnp.bfloat16


def iota(shape, axis):
    return lax.broadcasted_iota(jnp.int32, shape, axis)


def kernel(
    q_hbm, nk_hbm, nv_hbm, pt_hbm, len_hbm, k_hbm, v_hbm, w_hbm, out_ref,
    q_ref, nk_ref, nv_ref, pt_ref, len_ref, k_buf, v_buf, w_buf, pbuf, zq, tbuf, ubuf, sbuf, rbuf, zo, zs, abuf, xbuf,
    load_sem, send_sem, recv_sem, ready_sem,
):
    i = lax.axis_index("seq")
    x = lax.axis_index("mp")
    z = i // LOCAL
    p = lax.rem(i, LOCAL)

    z_steps = sorted(range(1, PLANES), key=lambda k: -min(k, PLANES - k))
    p_steps = ((2, 0), (2, 1), (1, 0), (3, 0), (1, 1), (3, 1), (0, 1))
    x_steps = (2, 1, 3)

    def z_peer(k):
        return {"seq": lax.rem(z + k, PLANES) * LOCAL + p}

    def p_index(k):
        return lax.rem((p >> 1) + k[0], 4) * 2 + lax.rem((p & 1) + k[1], 2)

    def p_peer(k):
        return {"seq": z * LOCAL + p_index(k)}

    def x_peer(k):
        return {"mp": lax.rem(x + k, XS)}

    peers = [z_peer(k) for k in z_steps if min(k, PLANES - k) <= 4]
    peers += [p_peer(k) for k in p_steps]
    peers += [x_peer(k) for k in x_steps]
    barrier = pltpu.get_barrier_semaphore()
    for peer in peers:
        pl.semaphore_signal(barrier, inc=1, device_id=peer, device_id_type=MESH)

    loads = [
        pltpu.make_async_copy(src, dst, load_sem.at[n])
        for n, (src, dst) in enumerate(
            (
                (q_hbm, q_ref), (pt_hbm, pt_ref), (len_hbm, len_ref), (nk_hbm, nk_ref),
                (nv_hbm, nv_ref), (k_hbm, k_buf), (v_hbm, v_buf), (w_hbm, w_buf),
            )
        )
    ]
    for load in loads:
        load.start()

    def send(src, dst, n, peer, m=None):
        pltpu.make_async_remote_copy(
            src_ref=src, dst_ref=dst, send_sem=send_sem.at[n], recv_sem=recv_sem.at[n if m is None else m],
            device_id=peer, device_id_type=MESH,
        ).start()

    def wait(ref, sems, n):
        pltpu.make_async_copy(ref, ref, sems.at[n]).wait()

    loads[0].wait()
    lane8 = iota((8, 128), 1)
    spread = (iota((32, 128), 0) == (iota((32, 128), 1) & 31)).astype(BF16)
    wide = jnp.dot(q_ref[...], spread, preferred_element_type=F32)
    pbuf[p] = jnp.where((lane8 >> 5) == (p & 3), wide, 0.0)

    pl.semaphore_wait(barrier, len(peers))
    for k in (4, 12):
        pl.semaphore_signal(ready_sem, inc=1, device_id=z_peer(k), device_id_type=MESH)
    for k in p_steps:
        send(pbuf.at[p], pbuf.at[p], 0, p_peer(k))

    for load in loads[1:5]:
        load.wait()
    lane64 = iota((128, 64), 1)
    rho = iota((128, 64), 0)
    my_slot = i * SLOTS + (rho >> 5)
    plane_slot = z * (LOCAL * SLOTS) + (rho >> 2)
    row_acc = jnp.zeros((128, 64), F32)
    live_acc = jnp.zeros((128, 64), F32)
    plane_acc = jnp.zeros((128, 64), F32)
    for r in range(ROWS):
        entry = pt_ref[r : r + 1, :]
        hit = entry == my_slot
        row_acc += jnp.where(hit, float(r), 0.0)
        live_acc += jnp.where(hit, (len_ref[r] - lane64 * PAGE).astype(F32), 0.0)
        plane_acc += jnp.where(entry == plane_slot, float(r), 0.0)
    row_of = jnp.sum(row_acc, axis=1, keepdims=True).astype(jnp.int32)
    live_of = jnp.sum(live_acc, axis=1, keepdims=True).astype(jnp.int32)
    plane_row = jnp.sum(plane_acc, axis=1, keepdims=True).astype(jnp.int32)

    rho1 = iota((128, 1), 0)
    tau1 = iota((32, 1), 0)
    head = jnp.concatenate([rho1 & 31, 4 * p + (tau1 >> 3)], axis=0)
    row = jnp.concatenate([row_of, tau1 & 7], axis=0)
    start = (head >> 1) * 16 + (head & 1) * 8 + row
    select = (iota((160, 256), 1) == start).astype(F32).astype(BF16)
    l0, l1 = iota((128, 128), 0), iota((128, 128), 1)
    match = ((l0 & 3) == ((l1 >> 3) & 3)) & (plane_row == (l1 & 7))
    first_kv = p < 4
    nk = jnp.where(first_kv, nk_ref[:, :HD].astype(F32), nk_ref[:, HD:].astype(F32))
    nv = jnp.where(first_kv, nv_ref[:, :HD].astype(F32), nv_ref[:, HD:].astype(F32))
    nk = jnp.concatenate([nk] * 4, axis=0)
    nv = jnp.concatenate([nv] * 4, axis=0)

    wait(pbuf.at[pl.ds(0, LOCAL - 1)], recv_sem, 0)
    low = (pbuf[0] + pbuf[1]) + (pbuf[2] + pbuf[3])
    high = (pbuf[4] + pbuf[5]) + (pbuf[6] + pbuf[7])
    zq[z] = jnp.concatenate([low, high], axis=0).astype(BF16)
    pl.semaphore_wait(ready_sem, 2)
    for k in z_steps:
        send(zq.at[z], zq.at[z], 1, z_peer(k))
    wait(zq.at[pl.ds(0, PLANES - 1)], recv_sem, 1)

    queries = jnp.dot(select, zq[...].reshape(256, 128), preferred_element_type=F32)
    fresh_queries = queries[128:]
    queries = queries[:128]

    scale = 1.0 / math.sqrt(HD)
    low_head = iota((32, HD), 0) < 16
    offset = iota((32, PAGE), 1)
    stat_lane = iota((32, HD), 1) < 64
    loads[5].wait()
    weights = []
    for s in range(SLOTS):
        mine = queries[32 * s : 32 * s + 32]
        block = jnp.concatenate(
            [jnp.where(low_head, mine, 0.0), jnp.where(low_head, 0.0, mine)], axis=1
        ).astype(BF16)
        scores = lax.dot_general(
            block, k_buf[s], (((1,), (1,)), ((), ())), preferred_element_type=F32
        )
        live = offset < live_of[32 * s : 32 * s + 32]
        masked = jnp.where(live, scores * scale, NEG)
        page_max = jnp.max(masked, axis=1, keepdims=True)
        weight = jnp.where(live, jnp.exp(masked - page_max), 0.0)
        weights.append(weight.astype(BF16))
        stats = jnp.where(stat_lane, page_max, jnp.sum(weight, axis=1, keepdims=True))
        for n in range(LOCAL):
            tbuf[n, 4 * s : 4 * s + 4, :] = stats[4 * n : 4 * n + 4]
    for k in p_steps:
        send(tbuf.at[p_index(k)], ubuf.at[p], 2, p_peer(k))
    ubuf[p] = tbuf[p]
    loads[6].wait()
    for s in range(SLOTS):
        outs = jnp.dot(weights[s], v_buf[s], preferred_element_type=F32)
        for n in range(LOCAL):
            half = n // 4
            sbuf[n, 4 * s : 4 * s + 4, :] = outs[4 * n : 4 * n + 4, half * HD : (half + 1) * HD]
    for k in p_steps:
        send(sbuf.at[p_index(k)], rbuf.at[p], 3, p_peer(k))
    rbuf[p] = sbuf[p]
    fresh_scores = jnp.sum(fresh_queries * nk, axis=1, keepdims=True) * scale

    wait(ubuf.at[pl.ds(0, LOCAL - 1)], recv_sem, 2)
    stats = ubuf[...].reshape(128, 128)
    turned = pltpu.roll(stats, 64, 1)
    part_max = jnp.where(l1 < 64, stats, turned)
    part_total = jnp.where(l1 < 64, turned, stats)
    plane_max = jnp.max(jnp.where(match, part_max, NEG), axis=0, keepdims=True)
    factor = jnp.where(match, jnp.exp(part_max - plane_max), 0.0)
    plane_total = jnp.sum(factor * part_total, axis=0, keepdims=True)
    lane1 = iota((1, 128), 1)
    zs[z] = jnp.where(lane1 < 32, plane_max, plane_total)
    for k in z_steps:
        send(zs.at[z], zs.at[z], 4, z_peer(k))
    factor = factor.T[:32]
    wait(rbuf.at[pl.ds(0, LOCAL - 1)], recv_sem, 3)
    merged = jnp.dot(
        factor, rbuf[...].reshape(128, 128), preferred_element_type=F32, precision=lax.Precision.HIGHEST
    )
    zo[z] = merged.astype(BF16)
    for k in z_steps:
        send(zo.at[z], zo.at[z], 5, z_peer(k))

    wait(zs.at[pl.ds(0, PLANES - 1)], recv_sem, 4)
    row16 = iota((16, 128), 0)
    table = jnp.zeros((PLANES, 128), F32)
    for n in range(PLANES):
        table = jnp.where(row16 == n, zs[n], table)
    table = jnp.concatenate([table, jnp.zeros((128 - PLANES, 128), F32)], axis=0).T
    lane32 = iota((32, 128), 1)
    maxima = jnp.where(lane32 < PLANES, table[:32], NEG)
    totals = jnp.where(lane32 < PLANES, table[32:64], 0.0)
    top = jnp.maximum(jnp.max(maxima, axis=1, keepdims=True), fresh_scores)
    factor = jnp.exp(maxima - top)
    fresh_factor = jnp.exp(fresh_scores - top)
    total = jnp.sum(factor * totals, axis=1, keepdims=True) + fresh_factor
    shares = [
        jnp.broadcast_to(factor[:, n : n + 1], (32, 128)) for n in range(PLANES)
    ]
    mixed = fresh_factor * nv
    wait(zo.at[pl.ds(0, PLANES - 1)], recv_sem, 5)
    for n in range(PLANES):
        mixed += shares[n] * zo[n].astype(F32)
    abuf[p] = (mixed / total).astype(BF16)
    for n, k in enumerate(p_steps):
        send(abuf.at[p], abuf.at[p], 6, p_peer(k), 8 + n)

    def project(n):
        block = abuf[n].astype(F32)
        flat = jnp.concatenate([block[8 * h : 8 * h + 8] for h in range(4)], axis=1).astype(BF16)
        rows = pl.ds(pl.multiple_of(n * 512, 512), 512)
        return jnp.dot(flat, w_buf[rows, :], preferred_element_type=F32)

    loads[7].wait()
    acc = project(p)
    for n, k in reversed(tuple(enumerate(p_steps))):
        source = p_index((4 - k[0], k[1]))
        wait(abuf.at[source], recv_sem, 8 + n)
        acc += project(source)
    xbuf[x] = acc
    for k in x_steps:
        send(xbuf.at[x], xbuf.at[x], 7, x_peer(k))
    wait(xbuf.at[pl.ds(0, XS - 1)], recv_sem, 7)
    out_ref[...] = ((xbuf[0] + xbuf[1]) + (xbuf[2] + xbuf[3])).astype(out_ref.dtype)

    wait(pbuf.at[pl.ds(0, LOCAL - 1)], send_sem, 0)
    wait(zq.at[pl.ds(0, PLANES - 1)], send_sem, 1)
    wait(ubuf.at[pl.ds(0, LOCAL - 1)], send_sem, 2)
    wait(rbuf.at[pl.ds(0, LOCAL - 1)], send_sem, 3)
    wait(zs.at[pl.ds(0, PLANES - 1)], send_sem, 4)
    wait(zo.at[pl.ds(0, PLANES - 1)], send_sem, 5)
    wait(abuf.at[pl.ds(0, LOCAL - 1)], send_sem, 6)
    wait(xbuf.at[pl.ds(0, XS - 1)], send_sem, 7)


def shards(queries, new_keys, new_values, keys, values, page_table, lengths, out_weight):
    operands = [
        pltpu.with_memory_space_constraint(a, pltpu.HBM)
        for a in (queries, new_keys, new_values, page_table, lengths, keys, values, out_weight)
    ]
    vmem = pl.BlockSpec(memory_space=pltpu.VMEM)
    hbm = pl.BlockSpec(memory_space=pl.ANY)
    return pl.pallas_call(
        kernel,
        out_shape=pltpu.VMEM((ROWS, out_weight.shape[1]), BF16),
        in_specs=[hbm] * 8,
        out_specs=vmem,
        scratch_shapes=[
            pltpu.VMEM(queries.shape, BF16),
            pltpu.VMEM(new_keys.shape, BF16),
            pltpu.VMEM(new_values.shape, BF16),
            pltpu.VMEM(page_table.shape, jnp.int32),
            pltpu.SMEM(lengths.shape, jnp.int32),
            pltpu.VMEM(keys.shape, BF16),
            pltpu.VMEM(values.shape, BF16),
            pltpu.VMEM(out_weight.shape, BF16),
            pltpu.VMEM((LOCAL, 8, 128), F32),
            pltpu.VMEM((PLANES, 16, 128), BF16),
            pltpu.VMEM((LOCAL, 16, 128), F32),
            pltpu.VMEM((LOCAL, 16, 128), F32),
            pltpu.VMEM((LOCAL, 16, 128), F32),
            pltpu.VMEM((LOCAL, 16, 128), F32),
            pltpu.VMEM((PLANES, 32, 128), BF16),
            pltpu.VMEM((PLANES, 1, 128), F32),
            pltpu.VMEM((LOCAL, 32, 128), BF16),
            pltpu.VMEM((XS, ROWS, 128), F32),
            pltpu.SemaphoreType.DMA((8,)),
            pltpu.SemaphoreType.DMA((8,)),
            pltpu.SemaphoreType.DMA((15,)),
            pltpu.SemaphoreType.REGULAR,
        ],
        compiler_params=pltpu.CompilerParams(
            collective_id=0, has_side_effects=True, vmem_limit_bytes=40 * 1024 * 1024
        ),
    )(*operands)


def solution(mesh):
    placed = (
        P(None, ("mp", "seq")),
        P(None, "mp"),
        P(None, "mp"),
        P("seq", None, "mp"),
        P("seq", None, "mp"),
        P(),
        P(),
        P("mp", "seq"),
    )
    return jax.shard_map(
        shards, mesh=mesh, in_specs=placed, out_specs=P(None, "seq"), check_vma=False
    )
```

```python
import math

import jax
import jax.numpy as jnp
from jax import lax
from jax.experimental import pallas as pl
from jax.experimental.pallas import tpu as pltpu
from jax.sharding import PartitionSpec as P

MESH = pl.DeviceIdType.MESH
NEG = -1e30
HD = 128
ROWS = 8
PLANES = 16
LOCAL = 8
XS = 4
SLOTS = 4
PAGE = 512
F32 = jnp.float32
BF16 = jnp.bfloat16


def iota(shape, axis):
    return lax.broadcasted_iota(jnp.int32, shape, axis)


def kernel(
    q_hbm, nk_hbm, nv_hbm, pt_hbm, len_hbm, k_hbm, v_hbm, w_hbm, out_ref,
    q_ref, nk_ref, nv_ref, pt_ref, len_ref, k_buf, v_buf, wp, pbuf, zq, tbuf, ubuf, sbuf, rbuf, zo, zs, hbuf, gbuf,
    load_sem, send_sem, recv_sem, ready_sem,
):
    i = lax.axis_index("seq")
    x = lax.axis_index("mp")
    z = i // LOCAL
    p = lax.rem(i, LOCAL)

    z_steps = sorted(range(1, PLANES), key=lambda k: -min(k, PLANES - k))
    p_steps = ((2, 0), (2, 1), (1, 0), (3, 0), (1, 1), (3, 1), (0, 1))
    g_steps = sorted(
        ((a, b, c) for a in range(4) for b in range(2) for c in range(XS) if a or b or c),
        key=lambda k: -min(k[0], 4 - k[0]) - min(k[2], XS - k[2]),
    )

    def z_peer(k):
        return {"seq": lax.rem(z + k, PLANES) * LOCAL + p}

    def p_index(k):
        return lax.rem((p >> 1) + k[0], 4) * 2 + lax.rem((p & 1) + k[1], 2)

    def p_peer(k):
        return {"seq": z * LOCAL + p_index(k)}

    def g_peer(k):
        return {"seq": z * LOCAL + p_index(k), "mp": lax.rem(x + k[2], XS)}

    peers = [z_peer(k) for k in z_steps if min(k, PLANES - k) <= 4]
    peers += [g_peer(k) for k in g_steps]
    barrier = pltpu.get_barrier_semaphore()
    for peer in peers:
        pl.semaphore_signal(barrier, inc=1, device_id=peer, device_id_type=MESH)

    loads = [
        pltpu.make_async_copy(src, dst, load_sem.at[n])
        for n, (src, dst) in enumerate(
            (
                (q_hbm, q_ref), (pt_hbm, pt_ref), (len_hbm, len_ref), (nk_hbm, nk_ref),
                (nv_hbm, nv_ref), (k_hbm, k_buf), (v_hbm, v_buf),
            )
        )
    ]
    for load in loads:
        load.start()

    def send(src, dst, n, peer):
        pltpu.make_async_remote_copy(
            src_ref=src, dst_ref=dst, send_sem=send_sem.at[n], recv_sem=recv_sem.at[n],
            device_id=peer, device_id_type=MESH,
        ).start()

    def wait(ref, sems, n):
        pltpu.make_async_copy(ref, ref, sems.at[n]).wait()

    loads[0].wait()
    lane8 = iota((8, 128), 1)
    spread = (iota((32, 128), 0) == (iota((32, 128), 1) & 31)).astype(BF16)
    wide = jnp.dot(q_ref[...], spread, preferred_element_type=F32)
    pbuf[p] = jnp.where((lane8 >> 5) == (p & 3), wide, 0.0)

    pl.semaphore_wait(barrier, len(peers))
    for k in (4, 12):
        pl.semaphore_signal(ready_sem, inc=1, device_id=z_peer(k), device_id_type=MESH)
    for k in p_steps:
        send(pbuf.at[p], pbuf.at[p], 0, p_peer(k))

    for load in loads[1:5]:
        load.wait()
    lane64 = iota((128, 64), 1)
    rho = iota((128, 64), 0)
    my_slot = i * SLOTS + (rho >> 5)
    plane_slot = z * (LOCAL * SLOTS) + (rho >> 2)
    row_acc = jnp.zeros((128, 64), F32)
    live_acc = jnp.zeros((128, 64), F32)
    plane_acc = jnp.zeros((128, 64), F32)
    for r in range(ROWS):
        entry = pt_ref[r : r + 1, :]
        hit = entry == my_slot
        row_acc += jnp.where(hit, float(r), 0.0)
        live_acc += jnp.where(hit, (len_ref[r] - lane64 * PAGE).astype(F32), 0.0)
        plane_acc += jnp.where(entry == plane_slot, float(r), 0.0)
    row_of = jnp.sum(row_acc, axis=1, keepdims=True).astype(jnp.int32)
    live_of = jnp.sum(live_acc, axis=1, keepdims=True).astype(jnp.int32)
    plane_row = jnp.sum(plane_acc, axis=1, keepdims=True).astype(jnp.int32)

    rho1 = iota((128, 1), 0)
    tau1 = iota((32, 1), 0)
    head = jnp.concatenate([rho1 & 31, 4 * p + (tau1 >> 3)], axis=0)
    row = jnp.concatenate([row_of, tau1 & 7], axis=0)
    start = (head >> 1) * 16 + (head & 1) * 8 + row
    select = (iota((160, 256), 1) == start).astype(F32).astype(BF16)
    l0, l1 = iota((128, 128), 0), iota((128, 128), 1)
    match = ((l0 & 3) == ((l1 >> 3) & 3)) & (plane_row == (l1 & 7))
    first_kv = p < 4
    nk = jnp.where(first_kv, nk_ref[:, :HD].astype(F32), nk_ref[:, HD:].astype(F32))
    nv = jnp.where(first_kv, nv_ref[:, :HD].astype(F32), nv_ref[:, HD:].astype(F32))
    nk = jnp.concatenate([nk] * 4, axis=0)
    nv = jnp.concatenate([nv] * 4, axis=0)

    wait(pbuf.at[pl.ds(0, LOCAL - 1)], recv_sem, 0)
    low = (pbuf[0] + pbuf[1]) + (pbuf[2] + pbuf[3])
    high = (pbuf[4] + pbuf[5]) + (pbuf[6] + pbuf[7])
    zq[z] = jnp.concatenate([low, high], axis=0).astype(BF16)
    pl.semaphore_wait(ready_sem, 2)
    for k in z_steps:
        send(zq.at[z], zq.at[z], 1, z_peer(k))
    def weight_rows(n):
        return w_hbm.at[pl.ds(pl.multiple_of(n * 512, 512), 512), :]

    own_rows = pltpu.make_async_copy(weight_rows(p), wp.at[p], load_sem.at[7])
    own_rows.start()
    for k in p_steps[2:]:
        send(weight_rows(p_index(k)), wp.at[p], 6, p_peer(k))
    wait(zq.at[pl.ds(0, PLANES - 1)], recv_sem, 1)

    queries = jnp.dot(select, zq[...].reshape(256, 128), preferred_element_type=F32)
    fresh_queries = queries[128:]
    queries = queries[:128]

    scale = 1.0 / math.sqrt(HD)
    low_head = iota((32, HD), 0) < 16
    offset = iota((32, PAGE), 1)
    stat_lane = iota((32, HD), 1) < 64
    loads[5].wait()
    weights = []
    for s in range(SLOTS):
        mine = queries[32 * s : 32 * s + 32]
        block = jnp.concatenate(
            [jnp.where(low_head, mine, 0.0), jnp.where(low_head, 0.0, mine)], axis=1
        ).astype(BF16)
        scores = lax.dot_general(
            block, k_buf[s], (((1,), (1,)), ((), ())), preferred_element_type=F32
        )
        live = offset < live_of[32 * s : 32 * s + 32]
        masked = jnp.where(live, scores * scale, NEG)
        page_max = jnp.max(masked, axis=1, keepdims=True)
        weight = jnp.where(live, jnp.exp(masked - page_max), 0.0)
        weights.append(weight.astype(BF16))
        stats = jnp.where(stat_lane, page_max, jnp.sum(weight, axis=1, keepdims=True))
        for n in range(LOCAL):
            tbuf[n, 4 * s : 4 * s + 4, :] = stats[4 * n : 4 * n + 4]
    for k in p_steps:
        send(tbuf.at[p_index(k)], ubuf.at[p], 2, p_peer(k))
    ubuf[p] = tbuf[p]
    loads[6].wait()
    for s in range(SLOTS):
        outs = jnp.dot(weights[s], v_buf[s], preferred_element_type=F32)
        for n in range(LOCAL):
            half = n // 4
            sbuf[n, 4 * s : 4 * s + 4, :] = outs[4 * n : 4 * n + 4, half * HD : (half + 1) * HD]
    for k in p_steps:
        send(sbuf.at[p_index(k)], rbuf.at[p], 3, p_peer(k))
    rbuf[p] = sbuf[p]
    fresh_scores = jnp.sum(fresh_queries * nk, axis=1, keepdims=True) * scale

    wait(ubuf.at[pl.ds(0, LOCAL - 1)], recv_sem, 2)
    stats = ubuf[...].reshape(128, 128)
    turned = pltpu.roll(stats, 64, 1)
    part_max = jnp.where(l1 < 64, stats, turned)
    part_total = jnp.where(l1 < 64, turned, stats)
    plane_max = jnp.max(jnp.where(match, part_max, NEG), axis=0, keepdims=True)
    factor = jnp.where(match, jnp.exp(part_max - plane_max), 0.0)
    plane_total = jnp.sum(factor * part_total, axis=0, keepdims=True)
    lane1 = iota((1, 128), 1)
    zs[z] = jnp.where(lane1 < 32, plane_max, plane_total)
    for k in z_steps:
        send(zs.at[z], zs.at[z], 4, z_peer(k))
    factor = factor.T[:32]
    wait(rbuf.at[pl.ds(0, LOCAL - 1)], recv_sem, 3)
    merged = jnp.dot(
        factor, rbuf[...].reshape(128, 128), preferred_element_type=F32, precision=lax.Precision.HIGHEST
    )
    zo[z] = merged.astype(BF16)
    for n in range(PLANES - 1):
        plane = n + jnp.where(z <= n, 1, 0)
        send(zo.at[z], zo.at[z], 5, {"seq": plane * LOCAL + p})

    for k in p_steps[:2]:
        send(weight_rows(p_index(k)), wp.at[p], 6, p_peer(k))

    wait(zs.at[pl.ds(0, PLANES - 1)], recv_sem, 4)
    row16 = iota((16, 128), 0)
    table = jnp.zeros((PLANES, 128), F32)
    for n in range(PLANES):
        table = jnp.where(row16 == n, zs[n], table)
    table = jnp.concatenate([table, jnp.zeros((128 - PLANES, 128), F32)], axis=0).T
    lane32 = iota((32, 128), 1)
    maxima = jnp.where(lane32 < PLANES, table[:32], NEG)
    totals = jnp.where(lane32 < PLANES, table[32:64], 0.0)
    top = jnp.maximum(jnp.max(maxima, axis=1, keepdims=True), fresh_scores)
    factor = jnp.exp(maxima - top)
    fresh_factor = jnp.exp(fresh_scores - top)
    total = jnp.sum(factor * totals, axis=1, keepdims=True) + fresh_factor
    shares = [
        jnp.broadcast_to(factor[:, n : n + 1], (32, 128)) for n in range(PLANES)
    ]
    mixed = fresh_factor * nv
    wait(zo.at[pl.ds(0, PLANES - 1)], recv_sem, 5)
    for n in range(PLANES):
        mixed += shares[n] * zo[n].astype(F32)
    mixed = mixed / total
    flat = jnp.concatenate([mixed[8 * h : 8 * h + 8] for h in range(4)], axis=1).astype(BF16)
    own_rows.wait()
    wait(wp.at[pl.ds(0, LOCAL - 1)], recv_sem, 6)
    for n in range(LOCAL):
        hbuf[n] = jnp.dot(flat, wp[n], preferred_element_type=F32)
    for k in g_steps:
        send(hbuf.at[p_index(k)], gbuf.at[x * LOCAL + p], 7, g_peer(k))
    gbuf[x * LOCAL + p] = hbuf[p]
    wait(gbuf.at[pl.ds(0, XS * LOCAL - 1)], recv_sem, 7)
    terms = [gbuf[n] for n in range(XS * LOCAL)]
    while len(terms) > 1:
        terms = [a + b for a, b in zip(terms[::2], terms[1::2])]
    out_ref[...] = terms[0].astype(out_ref.dtype)

    wait(pbuf.at[pl.ds(0, LOCAL - 1)], send_sem, 0)
    wait(zq.at[pl.ds(0, PLANES - 1)], send_sem, 1)
    wait(ubuf.at[pl.ds(0, LOCAL - 1)], send_sem, 2)
    wait(rbuf.at[pl.ds(0, LOCAL - 1)], send_sem, 3)
    wait(zs.at[pl.ds(0, PLANES - 1)], send_sem, 4)
    wait(zo.at[pl.ds(0, PLANES - 1)], send_sem, 5)
    wait(wp.at[pl.ds(0, LOCAL - 1)], send_sem, 6)
    wait(gbuf.at[pl.ds(0, XS * LOCAL - 1)], send_sem, 7)


def shards(queries, new_keys, new_values, keys, values, page_table, lengths, out_weight):
    operands = [
        pltpu.with_memory_space_constraint(a, pltpu.HBM)
        for a in (queries, new_keys, new_values, page_table, lengths, keys, values, out_weight)
    ]
    vmem = pl.BlockSpec(memory_space=pltpu.VMEM)
    hbm = pl.BlockSpec(memory_space=pl.ANY)
    return pl.pallas_call(
        kernel,
        out_shape=pltpu.VMEM((ROWS, out_weight.shape[1]), BF16),
        in_specs=[hbm] * 8,
        out_specs=vmem,
        scratch_shapes=[
            pltpu.VMEM(queries.shape, BF16),
            pltpu.VMEM(new_keys.shape, BF16),
            pltpu.VMEM(new_values.shape, BF16),
            pltpu.VMEM(page_table.shape, jnp.int32),
            pltpu.SMEM(lengths.shape, jnp.int32),
            pltpu.VMEM(keys.shape, BF16),
            pltpu.VMEM(values.shape, BF16),
            pltpu.VMEM((LOCAL, out_weight.shape[0] // LOCAL, out_weight.shape[1]), BF16),
            pltpu.VMEM((LOCAL, 8, 128), F32),
            pltpu.VMEM((PLANES, 16, 128), BF16),
            pltpu.VMEM((LOCAL, 16, 128), F32),
            pltpu.VMEM((LOCAL, 16, 128), F32),
            pltpu.VMEM((LOCAL, 16, 128), F32),
            pltpu.VMEM((LOCAL, 16, 128), F32),
            pltpu.VMEM((PLANES, 32, 128), BF16),
            pltpu.VMEM((PLANES, 1, 128), F32),
            pltpu.VMEM((LOCAL, ROWS, 128), F32),
            pltpu.VMEM((XS * LOCAL, ROWS, 128), F32),
            pltpu.SemaphoreType.DMA((8,)),
            pltpu.SemaphoreType.DMA((8,)),
            pltpu.SemaphoreType.DMA((8,)),
            pltpu.SemaphoreType.REGULAR,
        ],
        compiler_params=pltpu.CompilerParams(
            collective_id=0, has_side_effects=True, vmem_limit_bytes=40 * 1024 * 1024
        ),
    )(*operands)


def solution(mesh):
    placed = (
        P(None, ("mp", "seq")),
        P(None, "mp"),
        P(None, "mp"),
        P("seq", None, "mp"),
        P("seq", None, "mp"),
        P(),
        P(),
        P("mp", "seq"),
    )
    return jax.shard_map(
        shards, mesh=mesh, in_specs=placed, out_specs=P(None, "seq"), check_vma=False
    )
```

```python
import math

import jax
import jax.numpy as jnp
from jax import lax
from jax.experimental import pallas as pl
from jax.experimental.pallas import tpu as pltpu
from jax.sharding import PartitionSpec as P

MESH = pl.DeviceIdType.MESH
NEG = -1e30
HD = 128
ROWS = 8
PLANES = 16
LOCAL = 8
XS = 4
SLOTS = 4
PAGE = 512
F32 = jnp.float32
BF16 = jnp.bfloat16


def iota(shape, axis):
    return lax.broadcasted_iota(jnp.int32, shape, axis)


def kernel(
    q_hbm, nk_hbm, nv_hbm, pt_hbm, len_hbm, k_hbm, v_hbm, w_hbm, out_ref,
    q_ref, nk_ref, nv_ref, pt_ref, len_ref, k_buf, v_buf, wp, pbuf, zq, tbuf, ubuf, sbuf, rbuf, zo, zs, hbuf, gbuf,
    load_sem, send_sem, recv_sem, ready_sem,
):
    i = lax.axis_index("seq")
    x = lax.axis_index("mp")
    z = i // LOCAL
    p = lax.rem(i, LOCAL)

    z_steps = sorted(range(1, PLANES), key=lambda k: -min(k, PLANES - k))
    p_steps = ((2, 0), (2, 1), (1, 0), (3, 0), (1, 1), (3, 1), (0, 1))
    g_steps = sorted(
        ((a, b, c) for a in range(4) for b in range(2) for c in range(XS) if a or b or c),
        key=lambda k: -min(k[0], 4 - k[0]) - min(k[2], XS - k[2]),
    )

    def z_peer(k):
        return {"seq": lax.rem(z + k, PLANES) * LOCAL + p}

    def p_index(k):
        return lax.rem((p >> 1) + k[0], 4) * 2 + lax.rem((p & 1) + k[1], 2)

    def p_peer(k):
        return {"seq": z * LOCAL + p_index(k)}

    def g_peer(k):
        return {"seq": z * LOCAL + p_index(k), "mp": lax.rem(x + k[2], XS)}

    peers = [z_peer(k) for k in z_steps if min(k, PLANES - k) <= 4]
    peers += [g_peer(k) for k in g_steps]
    barrier = pltpu.get_barrier_semaphore()
    for peer in peers:
        pl.semaphore_signal(barrier, inc=1, device_id=peer, device_id_type=MESH)

    loads = [
        pltpu.make_async_copy(src, dst, load_sem.at[n])
        for n, (src, dst) in enumerate(
            (
                (q_hbm, q_ref), (pt_hbm, pt_ref), (len_hbm, len_ref), (nk_hbm, nk_ref),
                (nv_hbm, nv_ref), (k_hbm, k_buf), (v_hbm, v_buf),
            )
        )
    ]
    for load in loads:
        load.start()

    def send(src, dst, n, peer):
        pltpu.make_async_remote_copy(
            src_ref=src, dst_ref=dst, send_sem=send_sem.at[n], recv_sem=recv_sem.at[n],
            device_id=peer, device_id_type=MESH,
        ).start()

    def wait(ref, sems, n):
        pltpu.make_async_copy(ref, ref, sems.at[n]).wait()

    loads[0].wait()
    lane8 = iota((8, 128), 1)
    spread = (iota((32, 128), 0) == (iota((32, 128), 1) & 31)).astype(BF16)
    wide = jnp.dot(q_ref[...], spread, preferred_element_type=F32)
    pbuf[p] = jnp.where((lane8 >> 5) == (p & 3), wide, 0.0)

    pl.semaphore_wait(barrier, len(peers))
    for k in (4, 12):
        pl.semaphore_signal(ready_sem, inc=1, device_id=z_peer(k), device_id_type=MESH)
    for k in p_steps:
        send(pbuf.at[p], pbuf.at[p], 0, p_peer(k))

    for load in loads[1:5]:
        load.wait()
    lane64 = iota((128, 64), 1)
    rho = iota((128, 64), 0)
    my_slot = i * SLOTS + (rho >> 5)
    plane_slot = z * (LOCAL * SLOTS) + (rho >> 2)
    row_acc = jnp.zeros((128, 64), F32)
    live_acc = jnp.zeros((128, 64), F32)
    plane_acc = jnp.zeros((128, 64), F32)
    for r in range(ROWS):
        entry = pt_ref[r : r + 1, :]
        hit = entry == my_slot
        row_acc += jnp.where(hit, float(r), 0.0)
        live_acc += jnp.where(hit, (len_ref[r] - lane64 * PAGE).astype(F32), 0.0)
        plane_acc += jnp.where(entry == plane_slot, float(r), 0.0)
    row_of = jnp.sum(row_acc, axis=1, keepdims=True).astype(jnp.int32)
    live_of = jnp.sum(live_acc, axis=1, keepdims=True).astype(jnp.int32)
    plane_row = jnp.sum(plane_acc, axis=1, keepdims=True).astype(jnp.int32)

    rho1 = iota((128, 1), 0)
    tau1 = iota((32, 1), 0)
    head = jnp.concatenate([rho1 & 31, 4 * p + (tau1 >> 3)], axis=0)
    row = jnp.concatenate([row_of, tau1 & 7], axis=0)
    start = (head >> 1) * 16 + (head & 1) * 8 + row
    select = (iota((160, 256), 1) == start).astype(F32).astype(BF16)
    l0, l1 = iota((128, 128), 0), iota((128, 128), 1)
    match = ((l0 & 3) == ((l1 >> 3) & 3)) & (plane_row == (l1 & 7))
    first_kv = p < 4
    nk = jnp.where(first_kv, nk_ref[:, :HD].astype(F32), nk_ref[:, HD:].astype(F32))
    nv = jnp.where(first_kv, nv_ref[:, :HD].astype(F32), nv_ref[:, HD:].astype(F32))
    nk = jnp.concatenate([nk] * 4, axis=0)
    nv = jnp.concatenate([nv] * 4, axis=0)

    wait(pbuf.at[pl.ds(0, LOCAL - 1)], recv_sem, 0)
    low = (pbuf[0] + pbuf[1]) + (pbuf[2] + pbuf[3])
    high = (pbuf[4] + pbuf[5]) + (pbuf[6] + pbuf[7])
    zq[z] = jnp.concatenate([low, high], axis=0).astype(BF16)
    pl.semaphore_wait(ready_sem, 2)
    for k in z_steps:
        send(zq.at[z], zq.at[z], 1, z_peer(k))
    def weight_rows(n):
        return w_hbm.at[pl.ds(pl.multiple_of(n * 512, 512), 512), :]

    own_rows = pltpu.make_async_copy(weight_rows(p), wp.at[p], load_sem.at[7])
    own_rows.start()
    for k in p_steps[2:]:
        send(weight_rows(p_index(k)), wp.at[p], 6, p_peer(k))
    loads[5].wait()
    loads[6].wait()
    wait(zq.at[pl.ds(0, PLANES - 1)], recv_sem, 1)

    queries = jnp.dot(select, zq[...].reshape(256, 128), preferred_element_type=F32)
    fresh_queries = queries[128:]
    queries = queries[:128]

    scale = 1.0 / math.sqrt(HD)
    low_head = iota((32, HD), 0) < 16
    offset = iota((32, PAGE), 1)
    stat_lane = iota((32, HD), 1) < 64
    weights = []
    for s in range(SLOTS):
        mine = queries[32 * s : 32 * s + 32]
        block = jnp.concatenate(
            [jnp.where(low_head, mine, 0.0), jnp.where(low_head, 0.0, mine)], axis=1
        ).astype(BF16)
        scores = lax.dot_general(
            block, k_buf[s], (((1,), (1,)), ((), ())), preferred_element_type=F32
        )
        live = offset < live_of[32 * s : 32 * s + 32]
        masked = jnp.where(live, scores * scale, NEG)
        page_max = jnp.max(masked, axis=1, keepdims=True)
        weight = jnp.where(live, jnp.exp(masked - page_max), 0.0)
        weights.append(weight.astype(BF16))
        stats = jnp.where(stat_lane, page_max, jnp.sum(weight, axis=1, keepdims=True))
        for n in range(LOCAL):
            tbuf[n, 4 * s : 4 * s + 4, :] = stats[4 * n : 4 * n + 4]
    for k in p_steps:
        send(tbuf.at[p_index(k)], ubuf.at[p], 2, p_peer(k))
    ubuf[p] = tbuf[p]
    for s in range(SLOTS):
        outs = jnp.dot(weights[s], v_buf[s], preferred_element_type=F32)
        for n in range(LOCAL):
            half = n // 4
            sbuf[n, 4 * s : 4 * s + 4, :] = outs[4 * n : 4 * n + 4, half * HD : (half + 1) * HD]
    for k in p_steps:
        send(sbuf.at[p_index(k)], rbuf.at[p], 3, p_peer(k))
    rbuf[p] = sbuf[p]
    fresh_scores = jnp.sum(fresh_queries * nk, axis=1, keepdims=True) * scale

    wait(ubuf.at[pl.ds(0, LOCAL - 1)], recv_sem, 2)
    stats = ubuf[...].reshape(128, 128)
    turned = pltpu.roll(stats, 64, 1)
    part_max = jnp.where(l1 < 64, stats, turned)
    part_total = jnp.where(l1 < 64, turned, stats)
    plane_max = jnp.max(jnp.where(match, part_max, NEG), axis=0, keepdims=True)
    factor = jnp.where(match, jnp.exp(part_max - plane_max), 0.0)
    plane_total = jnp.sum(factor * part_total, axis=0, keepdims=True)
    lane1 = iota((1, 128), 1)
    zs[z] = jnp.where(lane1 < 32, plane_max, plane_total)
    for n in range(PLANES - 1):
        plane = n + jnp.where(z <= n, 1, 0)
        send(zs.at[z], zs.at[z], 4, {"seq": plane * LOCAL + p})
    factor = factor.T[:32]
    high = factor.astype(BF16)
    low = (factor - high.astype(F32)).astype(BF16)
    factor = jnp.concatenate([high, high, low], axis=1)
    wait(rbuf.at[pl.ds(0, LOCAL - 1)], recv_sem, 3)
    parts = rbuf[...].reshape(128, 128)
    high = parts.astype(BF16)
    low = (parts - high.astype(F32)).astype(BF16)
    merged = jnp.dot(
        factor, jnp.concatenate([high, low, high], axis=0), preferred_element_type=F32
    )
    zo[z] = merged.astype(BF16)
    for n in range(PLANES - 1):
        plane = n + jnp.where(z <= n, 1, 0)
        send(zo.at[z], zo.at[z], 5, {"seq": plane * LOCAL + p})

    for k in p_steps[:2]:
        send(weight_rows(p_index(k)), wp.at[p], 6, p_peer(k))

    wait(zs.at[pl.ds(0, PLANES - 1)], recv_sem, 4)
    row16 = iota((16, 128), 0)
    table = jnp.zeros((PLANES, 128), F32)
    for n in range(PLANES):
        table = jnp.where(row16 == n, zs[n], table)
    table = jnp.concatenate([table, jnp.zeros((128 - PLANES, 128), F32)], axis=0).T
    lane32 = iota((32, 128), 1)
    maxima = jnp.where(lane32 < PLANES, table[:32], NEG)
    totals = jnp.where(lane32 < PLANES, table[32:64], 0.0)
    top = jnp.maximum(jnp.max(maxima, axis=1, keepdims=True), fresh_scores)
    factor = jnp.exp(maxima - top)
    fresh_factor = jnp.exp(fresh_scores - top)
    total = jnp.sum(factor * totals, axis=1, keepdims=True) + fresh_factor
    shares = [
        jnp.broadcast_to(factor[:, n : n + 1], (32, 128)) for n in range(PLANES)
    ]
    mixed = fresh_factor * nv
    wait(zo.at[pl.ds(0, PLANES - 1)], recv_sem, 5)
    for n in range(PLANES):
        mixed += shares[n] * zo[n].astype(F32)
    mixed = mixed / total
    flat = jnp.concatenate([mixed[8 * h : 8 * h + 8] for h in range(4)], axis=1).astype(BF16)
    own_rows.wait()
    wait(wp.at[pl.ds(0, LOCAL - 1)], recv_sem, 6)
    me = (p >> 1) * 8 + x * 2 + 1 - (p & 1)
    for n in range(0, LOCAL, 2):
        pair = jnp.dot(
            flat, jnp.concatenate([wp[n], wp[n + 1]], axis=1), preferred_element_type=F32
        )
        hbuf[n] = pair[:, :128]
        hbuf[n + 1] = pair[:, 128:]
        for m in range(max(0, 4 * n - 1), 4 * n + 7):
            other = m + jnp.where(me <= m, 1, 0)
            column = (other >> 3) * 2 + 1 - (other & 1)
            peer = {"seq": z * LOCAL + column, "mp": (other >> 1) & 3}
            send(hbuf.at[column], gbuf.at[x * LOCAL + p], 7, peer)
    gbuf[x * LOCAL + p] = hbuf[p]
    wait(gbuf.at[pl.ds(0, XS * LOCAL - 1)], recv_sem, 7)
    terms = [gbuf[n] for n in range(XS * LOCAL)]
    while len(terms) > 1:
        terms = [a + b for a, b in zip(terms[::2], terms[1::2])]
    out_ref[...] = terms[0].astype(out_ref.dtype)

    wait(pbuf.at[pl.ds(0, LOCAL - 1)], send_sem, 0)
    wait(zq.at[pl.ds(0, PLANES - 1)], send_sem, 1)
    wait(ubuf.at[pl.ds(0, LOCAL - 1)], send_sem, 2)
    wait(rbuf.at[pl.ds(0, LOCAL - 1)], send_sem, 3)
    wait(zs.at[pl.ds(0, PLANES - 1)], send_sem, 4)
    wait(zo.at[pl.ds(0, PLANES - 1)], send_sem, 5)
    wait(wp.at[pl.ds(0, LOCAL - 1)], send_sem, 6)
    wait(gbuf.at[pl.ds(0, XS * LOCAL - 1)], send_sem, 7)


def shards(queries, new_keys, new_values, keys, values, page_table, lengths, out_weight):
    operands = [
        pltpu.with_memory_space_constraint(a, pltpu.HBM)
        for a in (queries, new_keys, new_values, page_table, lengths, keys, values, out_weight)
    ]
    vmem = pl.BlockSpec(memory_space=pltpu.VMEM)
    hbm = pl.BlockSpec(memory_space=pl.ANY)
    return pl.pallas_call(
        kernel,
        out_shape=pltpu.VMEM((ROWS, out_weight.shape[1]), BF16),
        in_specs=[hbm] * 8,
        out_specs=vmem,
        scratch_shapes=[
            pltpu.VMEM(queries.shape, BF16),
            pltpu.VMEM(new_keys.shape, BF16),
            pltpu.VMEM(new_values.shape, BF16),
            pltpu.VMEM(page_table.shape, jnp.int32),
            pltpu.SMEM(lengths.shape, jnp.int32),
            pltpu.VMEM(keys.shape, BF16),
            pltpu.VMEM(values.shape, BF16),
            pltpu.VMEM((LOCAL, out_weight.shape[0] // LOCAL, out_weight.shape[1]), BF16),
            pltpu.VMEM((LOCAL, 8, 128), F32),
            pltpu.VMEM((PLANES, 16, 128), BF16),
            pltpu.VMEM((LOCAL, 16, 128), F32),
            pltpu.VMEM((LOCAL, 16, 128), F32),
            pltpu.VMEM((LOCAL, 16, 128), F32),
            pltpu.VMEM((LOCAL, 16, 128), F32),
            pltpu.VMEM((PLANES, 32, 128), BF16),
            pltpu.VMEM((PLANES, 1, 128), F32),
            pltpu.VMEM((LOCAL, ROWS, 128), F32),
            pltpu.VMEM((XS * LOCAL, ROWS, 128), F32),
            pltpu.SemaphoreType.DMA((8,)),
            pltpu.SemaphoreType.DMA((8,)),
            pltpu.SemaphoreType.DMA((8,)),
            pltpu.SemaphoreType.REGULAR,
        ],
        compiler_params=pltpu.CompilerParams(
            collective_id=0, has_side_effects=True, vmem_limit_bytes=40 * 1024 * 1024
        ),
    )(*operands)


def solution(mesh):
    placed = (
        P(None, ("mp", "seq")),
        P(None, "mp"),
        P(None, "mp"),
        P("seq", None, "mp"),
        P("seq", None, "mp"),
        P(),
        P(),
        P("mp", "seq"),
    )
    return jax.shard_map(
        shards, mesh=mesh, in_specs=placed, out_specs=P(None, "seq"), check_vma=False
    )
```

```python
import math

import jax
import jax.numpy as jnp
from jax import lax
from jax.experimental import pallas as pl
from jax.experimental.pallas import tpu as pltpu
from jax.sharding import PartitionSpec as P

MESH = pl.DeviceIdType.MESH
NEG = -1e30
HD = 128
ROWS = 8
PLANES = 16
LOCAL = 8
XS = 4
SLOTS = 4
PAGE = 512
F32 = jnp.float32
BF16 = jnp.bfloat16


def iota(shape, axis):
    return lax.broadcasted_iota(jnp.int32, shape, axis)


def kernel(
    q_hbm, nk_hbm, nv_hbm, pt_hbm, len_hbm, k_hbm, v_hbm, w_hbm, out_ref,
    q_ref, nk_ref, nv_ref, pt_ref, len_ref, k_buf, v_buf, wp, pbuf, zq, tbuf, ubuf, sbuf, rbuf, zo, zs, hbuf, gbuf,
    load_sem, send_sem, recv_sem, ready_sem,
):
    i = lax.axis_index("seq")
    x = lax.axis_index("mp")
    z = i // LOCAL
    p = lax.rem(i, LOCAL)

    z_steps = sorted(range(1, PLANES), key=lambda k: -min(k, PLANES - k))
    p_steps = ((2, 0), (2, 1), (1, 0), (3, 0), (1, 1), (3, 1), (0, 1))
    g_steps = sorted(
        ((a, b, c) for a in range(4) for b in range(2) for c in range(XS) if a or b or c),
        key=lambda k: -min(k[0], 4 - k[0]) - min(k[2], XS - k[2]),
    )

    def z_peer(k):
        return {"seq": lax.rem(z + k, PLANES) * LOCAL + p}

    def p_index(k):
        return lax.rem((p >> 1) + k[0], 4) * 2 + lax.rem((p & 1) + k[1], 2)

    def p_peer(k):
        return {"seq": z * LOCAL + p_index(k)}

    def g_peer(k):
        return {"seq": z * LOCAL + p_index(k), "mp": lax.rem(x + k[2], XS)}

    peers = [z_peer(k) for k in z_steps if min(k, PLANES - k) <= 4]
    peers += [g_peer(k) for k in g_steps]
    barrier = pltpu.get_barrier_semaphore()
    for peer in peers:
        pl.semaphore_signal(barrier, inc=1, device_id=peer, device_id_type=MESH)

    loads = [
        pltpu.make_async_copy(src, dst, load_sem.at[n])
        for n, (src, dst) in enumerate(
            (
                (q_hbm, q_ref), (pt_hbm, pt_ref), (len_hbm, len_ref), (nk_hbm, nk_ref),
                (nv_hbm, nv_ref), (k_hbm, k_buf), (v_hbm, v_buf),
            )
        )
    ]
    for load in loads:
        load.start()

    def send(src, dst, n, peer):
        pltpu.make_async_remote_copy(
            src_ref=src, dst_ref=dst, send_sem=send_sem.at[n], recv_sem=recv_sem.at[n],
            device_id=peer, device_id_type=MESH,
        ).start()

    def wait(ref, sems, n):
        pltpu.make_async_copy(ref, ref, sems.at[n]).wait()

    loads[0].wait()
    lane8 = iota((8, 128), 1)
    spread = (iota((32, 128), 0) == (iota((32, 128), 1) & 31)).astype(BF16)
    wide = jnp.dot(q_ref[...], spread, preferred_element_type=F32)
    pbuf[p] = jnp.where((lane8 >> 5) == (p & 3), wide, 0.0)

    pl.semaphore_wait(barrier, len(peers))
    for k in (4, 12):
        pl.semaphore_signal(ready_sem, inc=1, device_id=z_peer(k), device_id_type=MESH)
    for k in p_steps:
        send(pbuf.at[p], pbuf.at[p], 0, p_peer(k))

    for load in loads[1:5]:
        load.wait()
    lane64 = iota((128, 64), 1)
    rho = iota((128, 64), 0)
    my_slot = i * SLOTS + (rho >> 5)
    plane_slot = z * (LOCAL * SLOTS) + (rho >> 2)
    row_acc = jnp.zeros((128, 64), F32)
    live_acc = jnp.zeros((128, 64), F32)
    plane_acc = jnp.zeros((128, 64), F32)
    for r in range(ROWS):
        entry = pt_ref[r : r + 1, :]
        hit = entry == my_slot
        row_acc += jnp.where(hit, float(r), 0.0)
        live_acc += jnp.where(hit, (len_ref[r] - lane64 * PAGE).astype(F32), 0.0)
        plane_acc += jnp.where(entry == plane_slot, float(r), 0.0)
    row_of = jnp.sum(row_acc, axis=1, keepdims=True).astype(jnp.int32)
    live_of = jnp.sum(live_acc, axis=1, keepdims=True).astype(jnp.int32)
    plane_row = jnp.sum(plane_acc, axis=1, keepdims=True).astype(jnp.int32)

    rho1 = iota((128, 1), 0)
    tau1 = iota((32, 1), 0)
    head = jnp.concatenate([rho1 & 31, 4 * p + (tau1 >> 3)], axis=0)
    row = jnp.concatenate([row_of, tau1 & 7], axis=0)
    start = (head >> 1) * 16 + (head & 1) * 8 + row
    select = (iota((160, 256), 1) == start).astype(F32).astype(BF16)
    l0, l1 = iota((128, 128), 0), iota((128, 128), 1)
    match = ((l0 & 3) == ((l1 >> 3) & 3)) & (plane_row == (l1 & 7))
    first_kv = p < 4
    nk = jnp.where(first_kv, nk_ref[:, :HD].astype(F32), nk_ref[:, HD:].astype(F32))
    nv = jnp.where(first_kv, nv_ref[:, :HD].astype(F32), nv_ref[:, HD:].astype(F32))
    nk = jnp.concatenate([nk] * 4, axis=0)
    nv = jnp.concatenate([nv] * 4, axis=0)

    wait(pbuf.at[pl.ds(0, LOCAL - 1)], recv_sem, 0)
    low = (pbuf[0] + pbuf[1]) + (pbuf[2] + pbuf[3])
    high = (pbuf[4] + pbuf[5]) + (pbuf[6] + pbuf[7])
    zq[z] = jnp.concatenate([low, high], axis=0).astype(BF16)
    pl.semaphore_wait(ready_sem, 2)
    for k in z_steps:
        send(zq.at[z], zq.at[z], 1, z_peer(k))
    def weight_rows(n):
        return w_hbm.at[pl.ds(pl.multiple_of(n * 512, 512), 512), :]

    own_rows = pltpu.make_async_copy(weight_rows(p), wp.at[p], load_sem.at[7])
    own_rows.start()
    for k in p_steps[2:]:
        send(weight_rows(p_index(k)), wp.at[p], 6, p_peer(k))
    loads[5].wait()
    loads[6].wait()
    wait(zq.at[pl.ds(0, PLANES - 1)], recv_sem, 1)

    queries = jnp.dot(select, zq[...].reshape(256, 128), preferred_element_type=F32)
    fresh_queries = queries[128:]
    queries = queries[:128]

    scale = 1.0 / math.sqrt(HD)
    low_head = iota((32, HD), 0) < 16
    offset = iota((32, PAGE), 1)
    stat_lane = iota((32, HD), 1) < 64
    weights = []
    for s in range(SLOTS):
        mine = queries[32 * s : 32 * s + 32]
        block = jnp.concatenate(
            [jnp.where(low_head, mine, 0.0), jnp.where(low_head, 0.0, mine)], axis=1
        ).astype(BF16)
        scores = lax.dot_general(
            block, k_buf[s], (((1,), (1,)), ((), ())), preferred_element_type=F32
        )
        live = offset < live_of[32 * s : 32 * s + 32]
        masked = jnp.where(live, scores * scale, NEG)
        page_max = jnp.max(masked, axis=1, keepdims=True)
        weight = jnp.where(live, jnp.exp(masked - page_max), 0.0)
        weights.append(weight.astype(BF16))
        stats = jnp.where(stat_lane, page_max, jnp.sum(weight, axis=1, keepdims=True))
        for n in range(LOCAL):
            tbuf[n, 4 * s : 4 * s + 4, :] = stats[4 * n : 4 * n + 4]
    for k in p_steps:
        send(tbuf.at[p_index(k)], ubuf.at[p], 2, p_peer(k))
    ubuf[p] = tbuf[p]
    for s in range(SLOTS):
        outs = jnp.dot(weights[s], v_buf[s], preferred_element_type=F32)
        for n in range(LOCAL):
            half = n // 4
            sbuf[n, 4 * s : 4 * s + 4, :] = outs[4 * n : 4 * n + 4, half * HD : (half + 1) * HD]
    for k in p_steps:
        send(sbuf.at[p_index(k)], rbuf.at[p], 3, p_peer(k))
    rbuf[p] = sbuf[p]
    fresh_scores = jnp.sum(fresh_queries * nk, axis=1, keepdims=True) * scale

    wait(ubuf.at[pl.ds(0, LOCAL - 1)], recv_sem, 2)
    stats = ubuf[...].reshape(128, 128)
    turned = pltpu.roll(stats, 64, 1)
    part_max = jnp.where(l1 < 64, stats, turned)
    part_total = jnp.where(l1 < 64, turned, stats)
    plane_max = jnp.max(jnp.where(match, part_max, NEG), axis=0, keepdims=True)
    factor = jnp.where(match, jnp.exp(part_max - plane_max), 0.0)
    plane_total = jnp.sum(factor * part_total, axis=0, keepdims=True)
    lane1 = iota((1, 128), 1)
    zs[z] = jnp.where(lane1 < 32, plane_max, plane_total)
    for n in range(PLANES - 1):
        plane = n + jnp.where(z <= n, 1, 0)
        send(zs.at[z], zs.at[z], 4, {"seq": plane * LOCAL + p})
    factor = factor.T[:32]
    high = factor.astype(BF16)
    low = (factor - high.astype(F32)).astype(BF16)
    factor = jnp.concatenate([high, high, low], axis=1)
    wait(rbuf.at[pl.ds(0, LOCAL - 1)], recv_sem, 3)
    parts = rbuf[...].reshape(128, 128)
    high = parts.astype(BF16)
    low = (parts - high.astype(F32)).astype(BF16)
    merged = jnp.dot(
        factor, jnp.concatenate([high, low, high], axis=0), preferred_element_type=F32
    )
    zo[z] = merged.astype(BF16)
    for n in range(PLANES - 1):
        plane = n + jnp.where(z <= n, 1, 0)
        send(zo.at[z], zo.at[z], 5, {"seq": plane * LOCAL + p})

    for k in p_steps[:2]:
        send(weight_rows(p_index(k)), wp.at[p], 6, p_peer(k))

    wait(zs.at[pl.ds(0, PLANES - 1)], recv_sem, 4)
    row16 = iota((16, 128), 0)
    table = jnp.zeros((PLANES, 128), F32)
    for n in range(PLANES):
        table = jnp.where(row16 == n, zs[n], table)
    table = jnp.concatenate([table, jnp.zeros((128 - PLANES, 128), F32)], axis=0).T
    lane32 = iota((32, 128), 1)
    maxima = jnp.where(lane32 < PLANES, table[:32], NEG)
    totals = jnp.where(lane32 < PLANES, table[32:64], 0.0)
    top = jnp.maximum(jnp.max(maxima, axis=1, keepdims=True), fresh_scores)
    factor = jnp.exp(maxima - top)
    fresh_factor = jnp.exp(fresh_scores - top)
    total = jnp.sum(factor * totals, axis=1, keepdims=True) + fresh_factor
    factor = factor / total
    shares = [
        jnp.broadcast_to(factor[:, n : n + 1], (32, 128)) for n in range(PLANES)
    ]
    mixed = (fresh_factor / total) * nv
    wait(zo.at[pl.ds(0, PLANES - 1)], recv_sem, 5)
    for n in range(PLANES):
        mixed += shares[n] * zo[n].astype(F32)
    flat = jnp.concatenate([mixed[8 * h : 8 * h + 8] for h in range(4)], axis=1).astype(BF16)
    own_rows.wait()
    wait(wp.at[pl.ds(0, LOCAL - 1)], recv_sem, 6)
    me = (p >> 1) * 8 + x * 2 + 1 - (p & 1)
    for n in range(0, LOCAL, 2):
        pair = jnp.dot(
            flat, jnp.concatenate([wp[n], wp[n + 1]], axis=1), preferred_element_type=F32
        )
        hbuf[n] = pair[:, :128]
        hbuf[n + 1] = pair[:, 128:]
        for m in range(max(0, 4 * n - 1), 4 * n + 7):
            other = m + jnp.where(me <= m, 1, 0)
            column = (other >> 3) * 2 + 1 - (other & 1)
            peer = {"seq": z * LOCAL + column, "mp": (other >> 1) & 3}
            send(hbuf.at[column], gbuf.at[x * LOCAL + p], 7, peer)
    gbuf[x * LOCAL + p] = hbuf[p]
    wait(gbuf.at[pl.ds(0, XS * LOCAL - 1)], recv_sem, 7)
    terms = [gbuf[n] for n in range(XS * LOCAL)]
    while len(terms) > 1:
        terms = [a + b for a, b in zip(terms[::2], terms[1::2])]
    out_ref[...] = terms[0].astype(out_ref.dtype)

    wait(pbuf.at[pl.ds(0, LOCAL - 1)], send_sem, 0)
    wait(zq.at[pl.ds(0, PLANES - 1)], send_sem, 1)
    wait(ubuf.at[pl.ds(0, LOCAL - 1)], send_sem, 2)
    wait(rbuf.at[pl.ds(0, LOCAL - 1)], send_sem, 3)
    wait(zs.at[pl.ds(0, PLANES - 1)], send_sem, 4)
    wait(zo.at[pl.ds(0, PLANES - 1)], send_sem, 5)
    wait(wp.at[pl.ds(0, LOCAL - 1)], send_sem, 6)
    wait(gbuf.at[pl.ds(0, XS * LOCAL - 1)], send_sem, 7)


def shards(queries, new_keys, new_values, keys, values, page_table, lengths, out_weight):
    operands = [
        pltpu.with_memory_space_constraint(a, pltpu.HBM)
        for a in (queries, new_keys, new_values, page_table, lengths, keys, values, out_weight)
    ]
    vmem = pl.BlockSpec(memory_space=pltpu.VMEM)
    hbm = pl.BlockSpec(memory_space=pl.ANY)
    return pl.pallas_call(
        kernel,
        out_shape=pltpu.VMEM((ROWS, out_weight.shape[1]), BF16),
        in_specs=[hbm] * 8,
        out_specs=vmem,
        scratch_shapes=[
            pltpu.VMEM(queries.shape, BF16),
            pltpu.VMEM(new_keys.shape, BF16),
            pltpu.VMEM(new_values.shape, BF16),
            pltpu.VMEM(page_table.shape, jnp.int32),
            pltpu.SMEM(lengths.shape, jnp.int32),
            pltpu.VMEM(keys.shape, BF16),
            pltpu.VMEM(values.shape, BF16),
            pltpu.VMEM((LOCAL, out_weight.shape[0] // LOCAL, out_weight.shape[1]), BF16),
            pltpu.VMEM((LOCAL, 8, 128), F32),
            pltpu.VMEM((PLANES, 16, 128), BF16),
            pltpu.VMEM((LOCAL, 16, 128), F32),
            pltpu.VMEM((LOCAL, 16, 128), F32),
            pltpu.VMEM((LOCAL, 16, 128), F32),
            pltpu.VMEM((LOCAL, 16, 128), F32),
            pltpu.VMEM((PLANES, 32, 128), BF16),
            pltpu.VMEM((PLANES, 1, 128), F32),
            pltpu.VMEM((LOCAL, ROWS, 128), F32),
            pltpu.VMEM((XS * LOCAL, ROWS, 128), F32),
            pltpu.SemaphoreType.DMA((8,)),
            pltpu.SemaphoreType.DMA((8,)),
            pltpu.SemaphoreType.DMA((8,)),
            pltpu.SemaphoreType.REGULAR,
        ],
        compiler_params=pltpu.CompilerParams(
            collective_id=0, has_side_effects=True, vmem_limit_bytes=40 * 1024 * 1024
        ),
    )(*operands)


def solution(mesh):
    placed = (
        P(None, ("mp", "seq")),
        P(None, "mp"),
        P(None, "mp"),
        P("seq", None, "mp"),
        P("seq", None, "mp"),
        P(),
        P(),
        P("mp", "seq"),
    )
    return jax.shard_map(
        shards, mesh=mesh, in_specs=placed, out_specs=P(None, "seq"), check_vma=False
    )
```
